512 devices in a mesh: grp: 8 (over y, core), mem: 64 (over x, z).
Axes of the slice: x: 4, y: 4, z: 16, core: 2. Of those that a mesh axis runs over, the one named last changes fastest.
Arguments:
- tokens: bfloat16 [65536, 1024], P(('grp', 'mem')), may hold values from -6 to 6
- cotangent: bfloat16 [65536, 1024], P(('grp', 'mem')), may hold values from -6 to 6
- path: int32 [512, 3], P(('grp', 'mem')), may hold values from 0 to 1023, as said below
- coarse_weights: bfloat16 [4, 1024, 512], P(None, 'mem'), may hold values from -0.1875 to 0.1875
- middle_weights: bfloat16 [64, 1024, 256], P(None, 'mem'), may hold values from -0.1875 to 0.1875
- fine_weights: bfloat16 [1024, 1024, 128], P('grp', 'mem'), may hold values from -0.1875 to 0.1875
Outputs:
- tokens_grad: bfloat16 [65536, 1024], P(('grp', 'mem'))
- coarse_grad: bfloat16 [4, 1024, 512], P(None, 'mem')
- middle_grad: bfloat16 [64, 1024, 256], P(None, 'mem')
- fine_grad: bfloat16 [1024, 1024, 128], P('grp', 'mem')
The draws below stay inside these ranges and needn't reach their ends.
Inputs may be any that keep to these rules, and one draw needn't show every extreme that they name: Row d is the path of document d: column 0 its coarse block, column 1 its middle block, column 2 its fine block, with middle = fine * 64 // 1024 and coarse = middle * 4 // 64. Some fine blocks are chosen by many documents.
All inputs are finite; a program needn't handle non-finite values.
Results may differ from the reference program's by a relative error of at most 0.005.
Values may be sent and summed in bfloat16 or wider, within the bound.
No kernel may reach another device: no remote copies, remote signals or barrier semaphores. Data moves between devices by JAX's collectives and lax.ppermute only.
A program may use at most 64 MiB of HBM per device.

```python
from functools import partial
import jax
import jax.numpy as jnp
from jax import lax

D = 1024
HC = 256
HM = 128
HF = 64
COARSE = 4
MIDDLE = 64
TOK_DEV = 128
FINE = 1024
DOCS = 512
TOKENS = 65536


def draw_path(key, part):
    first, second, third, fourth = jax.random.split(key, 4)
    fine_ids = jax.random.randint(first, (DOCS,), 0, FINE)
    popular = jax.random.randint(second, (8,), 0, FINE)
    chooser = jax.random.randint(third, (DOCS,), 0, 32)
    fine_ids = jnp.where(chooser < 8, popular[chooser % 8], fine_ids)
    places = jax.random.permutation(fourth, DOCS)
    fine_ids = fine_ids.at[places[0]].set(0).at[places[1]].set(FINE - 1)
    middle_ids = fine_ids * MIDDLE // FINE
    coarse_ids = middle_ids * COARSE // MIDDLE
    return jnp.stack([coarse_ids, middle_ids, fine_ids], axis=1).astype(jnp.int32)


def steps_of(stream_key, dims, shards, smallest, top_value):
    def one(dim, shards_of):
        draws = jax.random.uniform(jax.random.fold_in(jax.random.fold_in(stream_key, 6), dim), (shards_of,), jnp.float32, smallest / len(shards), top_value / len(shards))
        return jnp.repeat(jnp.exp(draws), dims[dim] // shards_of).reshape((-1,) + (1,) * (len(dims) - dim - 1))

    loudness = one(*shards[0])
    for cut in shards[1:]:
        loudness = loudness * one(*cut)
    return loudness


def bell_draw(stream_key, dims, width, most, cuts=(), kind=jnp.bfloat16):
    entries = width * jax.random.normal(stream_key, dims, jnp.float32)
    if cuts:
        entries = entries * steps_of(stream_key, dims, cuts, -0.22, 0.18)
    return jnp.clip(entries, -most, most).astype(kind)


def setup_inputs(seed: int = 0) -> dict:
    streams_of = jax.random.split(jax.random.key(seed), 7)
    tokens = bell_draw(streams_of[0], (TOKENS, D), 1.0, 6.0, ((0, 512),))
    cotangent = bell_draw(streams_of[1], (TOKENS, D), 1.0, 6.0, ((0, 512),))
    path = draw_path(jax.random.fold_in(streams_of[6], 71), 0)
    coarse_weights = bell_draw(streams_of[3], (COARSE, D, 2 * HC), D ** -0.5, 0.1875, ((1, 64),))
    middle_weights = bell_draw(streams_of[4], (MIDDLE, D, 2 * HM), D ** -0.5, 0.1875, ((1, 64),))
    fine_weights = bell_draw(streams_of[5], (FINE, D, 2 * HF), D ** -0.5, 0.1875, ((0, 8), (1, 64)))
    return dict(tokens=tokens, cotangent=cotangent, path=path, coarse_weights=coarse_weights, middle_weights=middle_weights, fine_weights=fine_weights)


def contract_rows(left, right):
    return lax.dot_general(left, right, (((0,), (0,)), ((), ())), preferred_element_type=jnp.float32)

def level_terms(inputs, upstream, weights):
    hidden_width = weights.shape[1] // 2
    up_half = weights[:, :hidden_width]
    down_half = weights[:, hidden_width:]
    before = jnp.dot(inputs, up_half, preferred_element_type=jnp.float32)
    hidden, pullback = jax.vjp(partial(jax.nn.gelu, approximate=True), before)
    hidden_low = hidden.astype(jnp.bfloat16)
    hidden_grad = jnp.dot(upstream, down_half, preferred_element_type=jnp.float32)
    before_grad = pullback(hidden_grad)[0].astype(jnp.bfloat16)
    up_grad = contract_rows(inputs, before_grad)
    down_grad = contract_rows(upstream, hidden_low)
    input_part = lax.dot_general(before_grad, up_half, (((1,), (1,)), ((), ())), preferred_element_type=jnp.float32)
    return (jnp.concatenate([up_grad, down_grad], axis=1), input_part)

def reference(tokens, cotangent, path, coarse_weights, middle_weights, fine_weights):
    documents = path.shape[0]
    token_blocks = tokens.reshape(documents, TOK_DEV, D)
    upstream_blocks = cotangent.reshape(documents, TOK_DEV, D)
    start = (jnp.zeros(coarse_weights.shape, jnp.float32), jnp.zeros(middle_weights.shape, jnp.float32), jnp.zeros(fine_weights.shape, jnp.float32))

    def advance(carry, item):
        inputs, upstream, route = item
        coarse_sum, middle_sum, fine_sum = carry
        coarse_term, coarse_back = level_terms(inputs, upstream, coarse_weights[route[0]])
        middle_term, middle_back = level_terms(inputs, upstream, middle_weights[route[1]])
        fine_term, fine_back = level_terms(inputs, upstream, fine_weights[route[2]])
        coarse_sum = coarse_sum.at[route[0]].add(coarse_term)
        middle_sum = middle_sum.at[route[1]].add(middle_term)
        fine_sum = fine_sum.at[route[2]].add(fine_term)
        summed = (coarse_back + middle_back + fine_back).astype(jnp.bfloat16)
        return ((coarse_sum, middle_sum, fine_sum), summed)
    totals, input_grads = lax.scan(advance, start, (token_blocks, upstream_blocks, path))
    return (input_grads.reshape(documents * TOK_DEV, D), totals[0].astype(jnp.bfloat16), totals[1].astype(jnp.bfloat16), totals[2].astype(jnp.bfloat16))
```

```python
from functools import partial

import jax
import jax.numpy as jnp
from jax import lax
from jax.sharding import Mesh, PartitionSpec as P

F32 = jnp.float32
BF16 = jnp.bfloat16


def contract_rows(left, right):
    return lax.dot_general(
        left, right, (((0,), (0,)), ((), ())), preferred_element_type=F32
    )


def level_terms(inputs, upstream, weights):
    hidden_width = weights.shape[1] // 2
    up_half = weights[:, :hidden_width]
    down_half = weights[:, hidden_width:]
    before = jnp.dot(inputs, up_half, preferred_element_type=F32)
    hidden, pullback = jax.vjp(partial(jax.nn.gelu, approximate=True), before)
    hidden_low = hidden.astype(BF16)
    hidden_grad = jnp.dot(upstream, down_half, preferred_element_type=F32)
    before_grad = pullback(hidden_grad)[0].astype(BF16)
    up_grad = contract_rows(inputs, before_grad).astype(BF16)
    down_grad = contract_rows(upstream, hidden_low).astype(BF16)
    input_part = lax.dot_general(
        before_grad, up_half, (((1,), (1,)), ((), ())), preferred_element_type=F32
    )
    return (up_grad, down_grad, input_part)


def one_hot_rows(identity, count):
    return (identity[:, None] == jnp.arange(count, dtype=jnp.int32)[None, :]).astype(BF16)


def select_blocks(picker, blocks):
    return jnp.einsum("mk,krh->mrh", picker, blocks, preferred_element_type=F32).astype(BF16)


def collect_blocks(picker, pieces):
    return jnp.einsum("mk,mrh->krh", picker, pieces, preferred_element_type=F32)


def exchange(array, axes):
    return lax.all_to_all(array, axes, split_axis=0, concat_axis=0, tiled=True)


def gather(array, axes):
    count = lax.axis_size(axes)
    return exchange(jnp.broadcast_to(array[None], (count,) + array.shape), axes)


def on_device(tokens, cotangent, path, coarse_weights, middle_weights, fine_weights):
    y_count, c_count = lax.axis_size("y"), lax.axis_size("c")
    group_count = y_count * c_count
    member_count = lax.axis_size(("x", "z"))
    y_index, c_index = lax.axis_index("y"), lax.axis_index("c")
    group = y_index * c_count + c_index
    row_count = coarse_weights.shape[1]
    fine_owned, _, fine_width = fine_weights.shape
    coarse_count, _, coarse_width = coarse_weights.shape
    middle_count, _, middle_width = middle_weights.shape

    ids = gather(path[0], ("y", "c", "x", "z"))
    ids = ids.reshape(group_count, member_count, 3)
    own = lax.dynamic_index_in_dim(ids, group, 0, keepdims=False)
    coarse_pick = one_hot_rows(own[:, 0], coarse_count)
    middle_pick = one_hot_rows(own[:, 1], middle_count)
    fine_all = ids[:, :, 2].reshape(y_count, c_count, member_count)

    offsets = jnp.swapaxes(fine_all, 0, 1).reshape(-1) - group * fine_owned
    fine_send = select_blocks(one_hot_rows(offsets, fine_owned), fine_weights)
    fine_send = fine_send.reshape(c_count, y_count * member_count, row_count, fine_width)
    arrived = exchange(fine_send, "c")
    arrived = (arrived[0] + arrived[1]).reshape(y_count, member_count, row_count, fine_width)
    arrived = exchange(arrived, "y")
    fine_rows = (arrived[0] + arrived[1]) + (arrived[2] + arrived[3])

    blocks = jnp.concatenate(
        [
            select_blocks(coarse_pick, coarse_weights),
            select_blocks(middle_pick, middle_weights),
            fine_rows,
        ],
        axis=2,
    )
    mine = exchange(blocks, ("x", "z")).reshape(member_count * row_count, -1)

    low, high = coarse_width, coarse_width + middle_width
    c_up, c_down, c_back = level_terms(tokens, cotangent, mine[:, :low])
    m_up, m_down, m_back = level_terms(tokens, cotangent, mine[:, low:high])
    f_up, f_down, f_back = level_terms(tokens, cotangent, mine[:, high:])
    tokens_grad = (c_back + m_back + f_back).astype(BF16)
    terms = jnp.concatenate([c_up, c_down, m_up, m_down, f_up, f_down], axis=1)
    parts = exchange(terms.reshape(member_count, row_count, -1), ("x", "z"))

    coarse_local = collect_blocks(coarse_pick, parts[:, :, :low])
    middle_local = collect_blocks(middle_pick, parts[:, :, low:high])
    fine_parts = parts[:, :, high:]
    def cut(array):
        return jnp.concatenate(jnp.split(array, array.shape[2] // fine_width, axis=2), axis=0)

    def join(array, width):
        return jnp.concatenate(jnp.split(array, width // fine_width, axis=0), axis=2)

    local = jnp.concatenate([cut(middle_local), cut(coarse_local)], axis=0).astype(BF16)
    unit = local.shape[1:]

    def with_fine(shares, fine):
        copies = jnp.broadcast_to(fine[None], shares.shape[:1] + fine.shape)
        return jnp.concatenate([shares, copies], axis=1)

    shares = local.reshape((c_count, -1) + unit)
    count = shares.shape[1]
    two = exchange(with_fine(shares, fine_parts), "c")
    half = (two[0, :count].astype(F32) + two[1, :count].astype(F32)).astype(BF16)
    fine_both = two[:, count:].reshape((-1,) + unit)
    shares = half.reshape((y_count, -1) + unit)
    count = shares.shape[1]
    four = exchange(with_fine(shares, fine_both), "y")
    done = jnp.sum(four[:, :count], axis=0, dtype=F32).astype(BF16)
    fine_four = four[:, count:].reshape((-1,) + unit)
    total = gather(gather(done, "y"), "c").reshape(local.shape)
    fine_offsets = fine_all.reshape(-1) - group * fine_owned
    fine_total = collect_blocks(one_hot_rows(fine_offsets, fine_owned), fine_four)
    units = middle_count * (middle_width // fine_width)
    middle_total = join(total[:units], middle_width)
    coarse_total = join(total[units:], coarse_width)
    return (tokens_grad, coarse_total, middle_total, fine_total.astype(BF16))


def solution(mesh):
    fine_mesh = Mesh(mesh.devices.reshape(4, 2, 4, 16), ("y", "c", "x", "z"))
    everyone = ("y", "c", "x", "z")
    members = ("x", "z")
    return jax.shard_map(
        on_device,
        mesh=fine_mesh,
        in_specs=(
            P(everyone, None),
            P(everyone, None),
            P(everyone, None),
            P(None, members, None),
            P(None, members, None),
            P(("y", "c"), members, None),
        ),
        out_specs=(
            P(everyone, None),
            P(None, members, None),
            P(None, members, None),
            P(("y", "c"), members, None),
        ),
        check_vma=False,
    )
```

```python
from functools import partial

import jax
import jax.numpy as jnp
from jax import lax
from jax.experimental import pallas as pl
from jax.experimental.pallas import tpu as pltpu
from jax.sharding import Mesh, PartitionSpec as P

F32 = jnp.float32
BF16 = jnp.bfloat16
I32 = jnp.int32
Y, C, X, Z = 4, 2, 4, 16
MEMBERS = X * Z
ROWS = 16
EVERYONE = ("y", "c", "x", "z")


def contract_rows(left, right):
    return lax.dot_general(
        left, right, (((0,), (0,)), ((), ())), preferred_element_type=F32
    )


def level_terms(inputs, upstream, weights):
    hidden_width = weights.shape[1] // 2
    up_half = weights[:, :hidden_width]
    down_half = weights[:, hidden_width:]
    before = jnp.dot(inputs, up_half, preferred_element_type=F32)
    hidden, pullback = jax.vjp(partial(jax.nn.gelu, approximate=True), before)
    hidden_low = hidden.astype(BF16)
    hidden_grad = jnp.dot(upstream, down_half, preferred_element_type=F32)
    before_grad = pullback(hidden_grad)[0].astype(BF16)
    up_grad = contract_rows(inputs, before_grad)
    down_grad = contract_rows(upstream, hidden_low)
    input_part = lax.dot_general(
        before_grad, up_half, (((1,), (1,)), ((), ())), preferred_element_type=F32
    )
    return (up_grad, down_grad, input_part)


def one_hot_rows(identity, count):
    return (identity[:, None] == jnp.arange(count, dtype=I32)[None, :]).astype(BF16)


def collect_blocks(picker, pieces):
    return jnp.einsum("mk,mrh->krh", picker, pieces, preferred_element_type=F32)


def exchange(array, axes):
    return lax.all_to_all(array, axes, split_axis=0, concat_axis=0, tiled=True)


def gather(array, axes):
    count = lax.axis_size(axes)
    return exchange(jnp.broadcast_to(array[None], (count,) + array.shape), axes)


def shift(array, axis, step):
    count = lax.axis_size(axis)
    return lax.ppermute(array, axis, [(i, (i + step) % count) for i in range(count)])


def pick_kernel(ids_ref, middle_ref, own_ref, other_ref, out_ref):
    def step(m, carry):
        middle_id, slot, same = ids_ref[0, m], ids_ref[1, m], ids_ref[2, m]
        out_ref[m, :, : middle_ref.shape[2]] = middle_ref[middle_id]
        out_ref[m, :, middle_ref.shape[2] :] = jnp.where(
            same == 1, own_ref[slot], other_ref[slot]
        )
        return carry

    lax.fori_loop(0, MEMBERS, step, 0, unroll=8)


def pick(ids, middle, own, other):
    vmem = pl.BlockSpec(memory_space=pltpu.VMEM)
    return pl.pallas_call(
        pick_kernel,
        out_shape=jax.ShapeDtypeStruct(
            (MEMBERS, ROWS, middle.shape[2] + own.shape[2]), BF16
        ),
        in_specs=[pl.BlockSpec(memory_space=pltpu.SMEM), vmem, vmem, vmem],
        out_specs=vmem,
        compiler_params=pltpu.CompilerParams(vmem_limit_bytes=24 * 1024 * 1024),
    )(ids, middle, own, other)


def on_device(tokens, cotangent, path, coarse_weights, middle_weights, fine_weights):
    y_index, c_index = lax.axis_index("y"), lax.axis_index("c")
    x_index = lax.axis_index("x")
    group = y_index * C + c_index
    fine_owned, _, fine_width = fine_weights.shape
    coarse_count, _, coarse_width = coarse_weights.shape
    middle_count, _, middle_width = middle_weights.shape
    quarter = coarse_width // 4

    fine_own = jnp.concatenate(
        [fine_weights] + [shift(fine_weights, "y", s) for s in range(1, Y)], axis=0
    )
    fine_other = shift(fine_own, "c", 1)
    other_tokens = shift(tokens, "c", 1)
    other_cotangent = shift(cotangent, "c", 1)
    other_path = shift(path, "c", 1)

    mine_coarse = lax.dynamic_index_in_dim(coarse_weights, y_index, 0, keepdims=False)
    mine_coarse = jnp.concatenate(
        [
            lax.dynamic_slice_in_dim(mine_coarse, c_index * quarter, quarter, 1),
            lax.dynamic_slice_in_dim(mine_coarse, (c_index + 2) * quarter, quarter, 1),
        ],
        axis=1,
    )
    digits = jnp.stack([path[0, 1], path[0, 2] // 32, path[0, 2] % 32, path[0, 0]])
    line = gather(digits, "x").reshape(-1)
    line = jnp.zeros((8, 2 * quarter), I32).at[0, : line.shape[0]].set(line)
    packet = jnp.concatenate([mine_coarse, line.astype(BF16)], axis=0)
    packets = gather(packet, "z").reshape(Z, ROWS + 8, 2 * quarter)
    coarse_column = packets[:, :ROWS].reshape(Z * ROWS, 2 * quarter)
    numbers = packets[:, ROWS, : 4 * X].astype(I32).reshape(Z, X, 4)
    numbers = jnp.transpose(numbers, (2, 1, 0)).reshape(4, MEMBERS)
    middle_ids = numbers[0]
    fine_ids = numbers[1] * 32 + numbers[2]
    owner = fine_ids // fine_owned
    slots = ((y_index - owner // C) % Y) * fine_owned + fine_ids % fine_owned
    same = (owner % C == c_index).astype(I32)
    send = pick(jnp.stack([middle_ids, slots, same]), middle_weights, fine_own, fine_other)
    mine = exchange(send, ("x", "z")).reshape(MEMBERS * ROWS, -1)

    columns = jnp.stack([coarse_column] + [shift(coarse_column, "x", s) for s in range(1, X)])
    columns = jnp.stack([columns[(x_index - i) % X] for i in range(X)])
    half_block = columns.reshape(MEMBERS * ROWS, 2 * quarter)
    halves = jnp.stack([half_block] + [shift(half_block, "y", s) for s in range(1, Y)])
    own_id, other_id = path[0, 0], other_path[0, 0]
    own_half = halves[(y_index - own_id) % Y]
    other_half = halves[(y_index - other_id) % Y]
    a_up, a_down, a_back = level_terms(tokens, cotangent, own_half)
    b_up, b_down, b_back = level_terms(other_tokens, other_cotangent, other_half)
    own_term = jnp.concatenate([a_up, a_down], axis=1)
    other_term = jnp.concatenate([b_up, b_down], axis=1)

    def slot_of(block):
        both = jnp.where(own_id == block, own_term, 0.0) + jnp.where(
            other_id == block, other_term, 0.0
        )
        return both.astype(BF16)

    coarse_sum = slot_of(y_index).astype(F32)
    for s in range(1, Y):
        coarse_sum = coarse_sum + shift(slot_of((y_index + s) % Y), "y", s).astype(F32)
    coarse_sum = coarse_sum.astype(BF16)
    coarse_back = a_back + shift(b_back, "c", 1)

    m_up, m_down, m_back = level_terms(tokens, cotangent, mine[:, :middle_width])
    f_up, f_down, f_back = level_terms(tokens, cotangent, mine[:, middle_width:])
    tokens_grad = (coarse_back + m_back + f_back).astype(BF16)
    terms = [t.astype(BF16) for t in (m_up, m_down, f_up, f_down)]
    terms = jnp.concatenate(terms + [coarse_sum], axis=1)
    parts = exchange(terms.reshape(MEMBERS, ROWS, -1), ("x", "z"))

    def cut(array):
        return jnp.concatenate(jnp.split(array, array.shape[-1] // fine_width, axis=-1), axis=0)

    def join(array, width):
        return jnp.concatenate(jnp.split(array, width // fine_width, axis=0), axis=-1)

    coarse_done = jnp.sum(parts[:, :, middle_width + fine_width :], axis=0, dtype=F32)
    coarse_done = cut(coarse_done.astype(BF16)[None])
    middle_local = collect_blocks(
        one_hot_rows(middle_ids, middle_count), parts[:, :, :middle_width]
    )
    fine_parts = parts[:, :, middle_width : middle_width + fine_width]

    local = cut(middle_local).astype(BF16)
    unit = local.shape[1:]
    shares = local.reshape((C, -1) + unit)
    count = shares.shape[1]
    copies = jnp.broadcast_to(fine_parts[None], (C,) + fine_parts.shape)
    two = exchange(jnp.concatenate([shares, copies], axis=1), "c")
    half = (two[0, :count].astype(F32) + two[1, :count].astype(F32)).astype(BF16)
    fine_both = two[:, count:].reshape((-1,) + unit)
    all_ids = gather(fine_ids, "c").reshape(-1)
    fine_four = jnp.concatenate([fine_both] + [shift(fine_both, "y", s) for s in range(1, Y)])
    id_four = jnp.concatenate([all_ids] + [shift(all_ids, "y", s) for s in range(1, Y)])
    four = exchange(half.reshape((Y, -1) + unit), "y")
    done = jnp.sum(four, axis=0, dtype=F32).astype(BF16)
    done = jnp.concatenate([done, coarse_done], axis=0)
    total = gather(gather(done, "y"), "c").reshape((C, Y, done.shape[0]) + unit)
    fine_offsets = id_four - group * fine_owned
    fine_total = collect_blocks(one_hot_rows(fine_offsets, fine_owned), fine_four)
    middle_total = total[:, :, :-2].reshape(local.shape)
    middle_total = join(middle_total, middle_width)
    coarse_total = jnp.transpose(total[:, :, -2:], (1, 3, 2, 0, 4)).reshape(coarse_weights.shape)
    return (tokens_grad, coarse_total, middle_total, fine_total.astype(BF16))


def solution(mesh):
    fine_mesh = Mesh(mesh.devices.reshape(Y, C, X, Z), EVERYONE)
    members = ("x", "z")
    return jax.shard_map(
        on_device,
        mesh=fine_mesh,
        in_specs=(
            P(EVERYONE, None),
            P(EVERYONE, None),
            P(EVERYONE, None),
            P(None, members, None),
            P(None, members, None),
            P(("y", "c"), members, None),
        ),
        out_specs=(
            P(EVERYONE, None),
            P(None, members, None),
            P(None, members, None),
            P(("y", "c"), members, None),
        ),
        check_vma=False,
    )
```

```python
import jax
import jax.numpy as jnp
from jax import lax
from jax.experimental import pallas as pl
from jax.experimental.pallas import tpu as pltpu
from jax.sharding import Mesh, PartitionSpec as P

F32 = jnp.float32
BF16 = jnp.bfloat16
I32 = jnp.int32
Y, C, X, Z = 4, 2, 4, 16
MEMBERS = X * Z
ROWS = 16
EVERYONE = ("y", "c", "x", "z")
VMEM = pl.BlockSpec(memory_space=pltpu.VMEM)
SMEM = pl.BlockSpec(memory_space=pltpu.SMEM)


def exchange(array, axes):
    return lax.all_to_all(array, axes, split_axis=0, concat_axis=0, tiled=True)


def gather(array, axes):
    count = lax.axis_size(axes)
    return exchange(jnp.broadcast_to(array[None], (count,) + array.shape), axes)


def shift(array, axis, step):
    count = lax.axis_size(axis)
    return lax.ppermute(array, axis, [(i, (i + step) % count) for i in range(count)])


def after(array, *others):
    return lax.optimization_barrier((array,) + others)[0]


def kernel_call(body, in_specs, out_shape, scratch=(), cost=1_000_000, limit=16):
    return pl.pallas_call(
        body,
        out_shape=out_shape,
        in_specs=in_specs,
        out_specs=jax.tree.map(lambda _: VMEM, out_shape),
        scratch_shapes=list(scratch),
        compiler_params=pltpu.CompilerParams(vmem_limit_bytes=limit * 1024 * 1024),
        cost_estimate=pl.CostEstimate(flops=cost, bytes_accessed=cost, transcendentals=0),
    )


def bf16(*shape):
    return jax.ShapeDtypeStruct(shape, BF16)


def f32(*shape):
    return jax.ShapeDtypeStruct(shape, F32)


def dot(left, right, left_dim, right_dim):
    return lax.dot_general(
        left, right, (((left_dim,), (right_dim,)), ((), ())), preferred_element_type=F32
    )


def gelu_pair(v, upstream):
    scale = 0.7978845608028654
    square = v * v
    t = jnp.tanh(scale * (v + 0.044715 * (square * v)))
    half = 0.5 * (1.0 + t)
    slope = half + 0.5 * v * (1.0 - t * t) * (scale * (1.0 + 0.134145 * square))
    return (v * half).astype(BF16), (upstream * slope).astype(BF16)


def packet_kernel(where_ref, line_ref, coarse_ref, out_ref):
    y_index, c_index = where_ref[0], where_ref[1]
    width = coarse_ref.shape[2] // 4
    up = coarse_ref[y_index, :, pl.ds(pl.multiple_of(c_index * width, width), width)]
    down = coarse_ref[
        y_index, :, pl.ds(pl.multiple_of((c_index + 2) * width, width), width)
    ]
    lanes = lax.broadcasted_iota(I32, (ROWS, 128), 1)
    numbers = jnp.zeros((ROWS, 128), F32)
    for x in range(C * X):
        fine = line_ref[x, 0, 2]
        values = (line_ref[x, 0, 1], fine // 32, fine % 32)
        for i, value in enumerate(values):
            numbers = jnp.where(lanes == 4 * x + i, value.astype(F32), numbers)
    numbers = numbers.astype(BF16)
    for z in range(Z):
        out_ref[z, :, :width] = up
        out_ref[z, :, width : 2 * width] = down
        out_ref[z, :, 2 * width :] = numbers


def pick_kernel(where_ref, ids_ref, middle_ref, f0, f1, f2, f3, out_ref, other_ref):
    y_index, c_index = where_ref[0], where_ref[1]
    pieces = (f0, f1, f2, f3)
    owned = f0.shape[0]
    middle_width = middle_ref.shape[2]
    zeros = jnp.zeros(f0.shape[1:], BF16)

    def step(z, carry):
        for core in range(C):
            for x in range(X):
                place = 4 * (((core + c_index) % C) * X + x)
                fine_id = ids_ref[z, place + 1] * 32 + ids_ref[z, place + 2]
                owner = fine_id // owned
                choice = (y_index - owner // C + Y) % Y
                slot = fine_id % owned
                here = owner % C == c_index
                rows = zeros
                for s, piece in enumerate(pieces):
                    rows = jnp.where(jnp.logical_and(here, choice == s), piece[slot], rows)
                m = x * Z + z
                if core == 0:
                    out_ref[m, :, :middle_width] = middle_ref[ids_ref[z, place]]
                    out_ref[m, :, middle_width:] = rows
                else:
                    other_ref[m] = rows
        return carry

    lax.fori_loop(0, Z, step, 0, unroll=2)


def merge_kernel(send_ref, extra_ref, out_ref):
    middle_width = send_ref.shape[2] - extra_ref.shape[2]
    out_ref[:, :, :middle_width] = send_ref[:, :, :middle_width]
    out_ref[:, :, middle_width:] = send_ref[:, :, middle_width:] + extra_ref[...]


def coarse_kernel(
    where_ref, ids_ref, x_ref, g_ref, ox_ref, og_ref, h0, h1, h2, h3,
    s0, s1, s2, s3, back_ref, other_back_ref, half_ref, own_term, other_term,
):
    y_index = where_ref[0]
    c_index, x_index, z_index = where_ref[1], where_ref[2], where_ref[3]
    own_id = ids_ref[z_index, 4 * (c_index * X + x_index)] // 16
    other_id = ids_ref[z_index, 4 * ((1 - c_index) * X + x_index)] // 16
    width = h0.shape[1] // 2

    def level(identity, inputs, upstream, term_ref, into_ref):
        choice = (y_index - identity + Y) % Y
        for s, ref in enumerate((h0, h1, h2, h3)):

            @pl.when(choice == s)
            def _(ref=ref):
                half_ref[...] = ref[...]

        tokens, cotangent = inputs[...], upstream[...]
        before = dot(tokens, half_ref[:, :width], 1, 0)
        hidden_grad = dot(cotangent, half_ref[:, width:], 1, 0)
        hidden, before_grad = gelu_pair(before, hidden_grad)
        term_ref[:, :width] = dot(tokens, before_grad, 0, 0)
        term_ref[:, width:] = dot(cotangent, hidden, 0, 0)
        into_ref[...] = dot(before_grad, half_ref[:, :width], 1, 1)

    level(own_id, x_ref, g_ref, own_term, back_ref)
    level(other_id, ox_ref, og_ref, other_term, other_back_ref)
    for s, ref in enumerate((s0, s1, s2, s3)):
        block = (y_index + s) % Y
        own, other = own_id == block, other_id == block

        @pl.when(jnp.logical_and(own, other))
        def _(ref=ref):
            ref[...] = (own_term[...] + other_term[...]).astype(BF16)

        @pl.when(jnp.logical_and(own, jnp.logical_not(other)))
        def _(ref=ref):
            ref[...] = own_term[...].astype(BF16)

        @pl.when(jnp.logical_and(other, jnp.logical_not(own)))
        def _(ref=ref):
            ref[...] = other_term[...].astype(BF16)

        @pl.when(jnp.logical_not(jnp.logical_or(own, other)))
        def _(ref=ref):
            ref[...] = jnp.zeros(ref.shape, BF16)


def levels_kernel(x_ref, g_ref, w_ref, term_ref, back_ref):
    tokens, cotangent = x_ref[...], g_ref[...]
    middle = 256
    half = middle // 2
    before = dot(tokens, w_ref[:, :half], 1, 0)
    hidden_grad = dot(cotangent, w_ref[:, half:middle], 1, 0)
    hidden, before_grad = gelu_pair(before, hidden_grad)
    fine = w_ref[:, middle:]
    width = fine.shape[1]
    fine_before = dot(tokens, fine, 1, 0)
    fine_hidden_grad = pltpu.roll(dot(cotangent, fine, 1, 0), width // 2, 1)
    first = lax.broadcasted_iota(I32, fine_before.shape, 1) < width // 2
    fine_before = jnp.where(first, fine_before, 0.0)
    fine_hidden_grad = jnp.where(first, fine_hidden_grad, 0.0)
    fine_hidden, fine_before_grad = gelu_pair(fine_before, fine_hidden_grad)
    fine_hidden = pltpu.roll(fine_hidden.astype(F32), width // 2, 1).astype(BF16)
    term_ref[:, :half] = dot(tokens, before_grad, 0, 0).astype(BF16)
    term_ref[:, half:middle] = dot(cotangent, hidden, 0, 0).astype(BF16)
    term_ref[:, middle:] = (
        dot(tokens, fine_before_grad, 0, 0) + dot(cotangent, fine_hidden, 0, 0)
    ).astype(BF16)
    back_ref[...] = dot(before_grad, w_ref[:, :half], 1, 1) + dot(fine_before_grad, fine, 1, 1)


def collect_kernel(where_ref, ids_ref, parts_ref, keep_ref, send_ref, fine_ref, sums_ref):
    c_index = where_ref[1]
    middle = keep_ref.shape[2]
    half = keep_ref.shape[0]
    share = half // Y
    sums_ref[...] = jnp.zeros(sums_ref.shape, F32)

    def step(z, carry):
        for x in range(X):
            block = ids_ref[z, 4 * (c_index * X + x)]
            owner = block // share
            side = (owner + c_index) % C
            place = side * half + (owner // C) * share + block % share
            m = x * Z + z
            sums_ref[place] = sums_ref[place] + parts_ref[m, :, :middle].astype(F32)
            pair = (x % (X // 2)) * Z + z
            low = (x // (X // 2)) * 128
            fine_ref[pair, :, low : low + 128] = parts_ref[m, :, middle:]
        return carry

    lax.fori_loop(0, Z, step, 0, unroll=2)
    keep_ref[...] = sums_ref[:half].astype(BF16)
    send_ref[...] = sums_ref[half:].astype(BF16)


def fine_kernel(where_ref, ids_ref, *refs):
    pieces, out_ref, sums_ref = refs[:-2], refs[-2], refs[-1]
    group = where_ref[0] * C + where_ref[1]
    owned = out_ref.shape[0]
    sums_ref[...] = jnp.zeros(sums_ref.shape, F32)
    c_index = where_ref[1]
    for p, piece in enumerate(pieces):
        for core in range(C):

            def step(z, carry, p=p, core=core, piece=piece):
                for x in range(X):
                    place = 4 * (((core + c_index) % C) * X + x)
                    fine_id = ids_ref[p, z, place + 1] * 32 + ids_ref[p, z, place + 2]

                    @pl.when(fine_id // owned == group)
                    def _():
                        slot = fine_id % owned
                        pair = core * (MEMBERS // 2) + (x % (X // 2)) * Z + z
                        low = (x // (X // 2)) * 128
                        part = piece[pair, :, low : low + 128]
                        sums_ref[slot] = sums_ref[slot] + part.astype(F32)

                return carry

            lax.fori_loop(0, Z, step, 0, unroll=2)
    out_ref[...] = sums_ref[...].astype(BF16)


def on_device(tokens, cotangent, path, coarse_weights, middle_weights, fine_weights):
    y_index, c_index = lax.axis_index("y"), lax.axis_index("c")
    x_index = lax.axis_index("x")
    where = jnp.stack([y_index, c_index, x_index, lax.axis_index("z")]).astype(I32)
    fine_owned, _, fine_width = fine_weights.shape
    coarse_width = coarse_weights.shape[2]
    middle_width = middle_weights.shape[2]
    half = coarse_width // 2
    depth = MEMBERS * ROWS

    line = gather(path, ("c", "x"))
    packet = kernel_call(packet_kernel, [SMEM, SMEM, VMEM], bf16(Z, ROWS, half + 128))(
        where, line, coarse_weights
    )
    packets = exchange(packet, "z")

    fine_start = after(fine_weights, line)
    fine_rows = [fine_weights] + [shift(fine_start, "y", s) for s in range(1, Y)]
    both = jnp.concatenate([after(tokens, line), cotangent], axis=0)
    other_both = shift(both, "c", 1)
    *fine_rows, other_both = lax.optimization_barrier(fine_rows + [other_both])

    ids = packets[:, 0, half : half + 4 * C * X].astype(I32)
    send, extra = kernel_call(
        pick_kernel,
        [SMEM, SMEM, VMEM] + [VMEM] * Y,
        (bf16(MEMBERS, ROWS, middle_width + fine_width), bf16(MEMBERS, ROWS, fine_width)),
    )(where, ids, middle_weights, *fine_rows)
    send = kernel_call(merge_kernel, [VMEM] * 2, bf16(*send.shape))(send, shift(extra, "c", 1))
    mine = exchange(send, ("x", "z")).reshape(depth, -1)

    column = after(packets[:, :, :half].reshape(1, Z * ROWS, half), send)
    block = jnp.zeros((X, Z * ROWS, half), BF16)
    block = lax.dynamic_update_slice_in_dim(block, column, x_index, 0)
    for s in range(1, X):
        block = lax.dynamic_update_slice_in_dim(
            block, shift(column, "x", s), (x_index - s) % X, 0
        )
    block = block.reshape(depth, half)
    halves = [block] + [shift(block, "y", s) for s in range(1, Y)]
    length = tokens.shape[0]
    mine, *halves = lax.optimization_barrier([mine] + halves)
    slots = kernel_call(
        coarse_kernel,
        [SMEM, SMEM] + [VMEM] * 8,
        tuple([bf16(depth, half)] * Y + [f32(length, depth)] * 2),
        [
            pltpu.VMEM((depth, half), BF16),
            pltpu.VMEM((depth, half), F32),
            pltpu.VMEM((depth, half), F32),
        ],
        cost=20_000_000,
        limit=24,
    )(
        where, ids, tokens, cotangent, other_both[:length], other_both[length:], *halves
    )
    slots, coarse_back, other_back = slots[:Y], slots[Y], slots[Y + 1]

    terms, back = kernel_call(
        levels_kernel,
        [VMEM] * 3,
        (bf16(depth, middle_width + fine_width), f32(length, depth)),
        cost=10_000_000,
    )(tokens, cotangent, mine)
    parts = exchange(terms.reshape(MEMBERS, ROWS, -1), ("x", "z"))
    summed = slots[0].astype(F32)
    for s in range(1, Y):
        summed = summed + shift(after(slots[s], terms), "y", s).astype(F32)
    summed = summed.astype(BF16).reshape(X, Z * ROWS, half)
    column_sum = lax.dynamic_index_in_dim(summed, x_index, 0, keepdims=False).astype(F32)
    for s in range(1, X):
        leaving = lax.dynamic_index_in_dim(summed, (x_index + s) % X, 0, keepdims=False)
        column_sum = column_sum + shift(leaving, "x", s).astype(F32)
    column_sum = column_sum.astype(BF16).reshape(Z, ROWS, half)
    coarse_four = exchange(column_sum, "z")

    middle_count = middle_weights.shape[0]
    keep, leave, fine_pairs = kernel_call(
        collect_kernel,
        [SMEM, SMEM, VMEM],
        (
            bf16(middle_count // C, ROWS, middle_width),
            bf16(middle_count // C, ROWS, middle_width),
            bf16(MEMBERS // 2, ROWS, 2 * fine_width),
        ),
        [pltpu.VMEM((middle_count, ROWS, middle_width), F32)],
    )(where, ids, parts)
    numbers = jnp.pad(packets[None, :, 0, half:], ((0, 0), (0, ROWS - Z), (0, fine_width)))
    middle_half = keep.astype(F32) + shift(leave, "c", 1).astype(F32)
    middle_half = middle_half.astype(BF16).reshape(Y, -1, ROWS, middle_width)
    fine_both = jnp.concatenate([fine_pairs, shift(fine_pairs, "c", 1), numbers])
    middle_done = lax.dynamic_index_in_dim(middle_half, y_index, 0, keepdims=False).astype(F32)
    for s in range(1, Y):
        leaving = lax.dynamic_index_in_dim(middle_half, (y_index + s) % Y, 0, keepdims=False)
        middle_done = middle_done + shift(leaving, "y", s).astype(F32)
    fine_four = [fine_both] + [shift(fine_both, "y", s) for s in range(1, Y)]
    other_back = shift(after(other_back, middle_half), "c", 1)
    tokens_grad = (coarse_back + other_back + back).astype(BF16)
    coarse_four, middle_done = lax.optimization_barrier((coarse_four, middle_done))
    coarse_done = jnp.sum(coarse_four, axis=0, dtype=F32).astype(BF16)
    done = jnp.concatenate([middle_done.astype(BF16), coarse_done[None]], axis=0)
    total = gather(done, ("y", "c")).reshape((Y, C) + done.shape)
    middle_total = total[:, :, :-1].reshape(middle_weights.shape)
    coarse_total = total[:, :, -1].reshape(Y, C, ROWS, 2, half // 2)
    coarse_total = jnp.transpose(coarse_total, (0, 2, 3, 1, 4)).reshape(coarse_weights.shape)
    fine_ids = jnp.concatenate([f[MEMBERS:, :Z, : 4 * C * X] for f in fine_four]).astype(I32)
    fine_total = kernel_call(
        fine_kernel,
        [SMEM, SMEM] + [VMEM] * Y,
        bf16(fine_owned, ROWS, fine_width),
        [pltpu.VMEM((fine_owned, ROWS, fine_width), F32)],
    )(where, fine_ids, *fine_four)
    return (tokens_grad, coarse_total, middle_total, fine_total)


def solution(mesh):
    fine_mesh = Mesh(mesh.devices.reshape(Y, C, X, Z), EVERYONE)
    members = ("x", "z")
    return jax.shard_map(
        on_device,
        mesh=fine_mesh,
        in_specs=(
            P(EVERYONE, None),
            P(EVERYONE, None),
            P(EVERYONE, None),
            P(None, members, None),
            P(None, members, None),
            P(("y", "c"), members, None),
        ),
        out_specs=(
            P(EVERYONE, None),
            P(None, members, None),
            P(None, members, None),
            P(("y", "c"), members, None),
        ),
        check_vma=False,
    )
```

```python
import jax
import jax.numpy as jnp
from jax import lax
from jax.experimental import pallas as pl
from jax.experimental.pallas import tpu as pltpu
from jax.sharding import Mesh, PartitionSpec as P

F32 = jnp.float32
BF16 = jnp.bfloat16
I32 = jnp.int32
Y, C, X, Z = 4, 2, 4, 16
MEMBERS = X * Z
ROWS = 16
EVERYONE = ("y", "c", "x", "z")
VMEM = pl.BlockSpec(memory_space=pltpu.VMEM)
SMEM = pl.BlockSpec(memory_space=pltpu.SMEM)


def exchange(array, axes):
    return lax.all_to_all(array, axes, split_axis=0, concat_axis=0, tiled=True)


def gather(array, axes):
    count = lax.axis_size(axes)
    return exchange(jnp.broadcast_to(array[None], (count,) + array.shape), axes)


def shift(array, axis, step):
    count = lax.axis_size(axis)
    return lax.ppermute(array, axis, [(i, (i + step) % count) for i in range(count)])


def after(array, *others):
    return lax.optimization_barrier((array,) + others)[0]


def kernel_call(body, in_specs, out_shape, scratch=(), cost=1_000_000, limit=16):
    return pl.pallas_call(
        body,
        out_shape=out_shape,
        in_specs=in_specs,
        out_specs=jax.tree.map(lambda _: VMEM, out_shape),
        scratch_shapes=list(scratch),
        compiler_params=pltpu.CompilerParams(vmem_limit_bytes=limit * 1024 * 1024),
        cost_estimate=pl.CostEstimate(flops=cost, bytes_accessed=cost, transcendentals=0),
    )


def bf16(*shape):
    return jax.ShapeDtypeStruct(shape, BF16)


def f32(*shape):
    return jax.ShapeDtypeStruct(shape, F32)


def dot(left, right, left_dim, right_dim):
    return lax.dot_general(
        left, right, (((left_dim,), (right_dim,)), ((), ())), preferred_element_type=F32
    )


def gelu_pair(v, upstream):
    scale = 0.7978845608028654
    square = v * v
    t = jnp.tanh(scale * (v + 0.044715 * (square * v)))
    half = 0.5 * (1.0 + t)
    slope = half + 0.5 * v * (1.0 - t * t) * (scale * (1.0 + 0.134145 * square))
    return (v * half).astype(BF16), (upstream * slope).astype(BF16)


def packet_kernel(where_ref, own_ref, other_ref, coarse_ref, out_ref):
    y_index, c_index = where_ref[0], where_ref[1]
    width = coarse_ref.shape[2] // 4
    up = coarse_ref[y_index, :, pl.ds(pl.multiple_of(c_index * width, width), width)]
    down = coarse_ref[
        y_index, :, pl.ds(pl.multiple_of((c_index + 2) * width, width), width)
    ]
    lanes = lax.broadcasted_iota(I32, (ROWS, 128), 1)
    numbers = jnp.zeros((ROWS, 128), F32)
    for core, ref in ((c_index, own_ref), (1 - c_index, other_ref)):
        values = (ref[0, 1], ref[0, 2] // 32, ref[0, 2] % 32)
        for i, value in enumerate(values):
            numbers = jnp.where(lanes == 4 * core + i, value.astype(F32), numbers)
    numbers = numbers.astype(BF16)
    for z in range(Z):
        out_ref[z, :, :width] = up
        out_ref[z, :, width : 2 * width] = down
        out_ref[z, :, 2 * width :] = numbers


def numbers_kernel(grid_ref, out_ref):
    width = grid_ref.shape[3] - 128
    rows = lax.broadcasted_iota(I32, (ROWS, 128), 0)
    total = jnp.zeros((ROWS, 128), F32)
    for x in range(X):
        line = jnp.zeros((ROWS, 128), F32)
        for z in range(Z):
            line = jnp.where(rows == z, grid_ref[x, z, :, width:].astype(F32), line)
        total = total + (pltpu.roll(line, 8 * x, 1) if x else line)
    out_ref[0, :, :128] = total.astype(BF16)
    out_ref[0, :, 128:] = jnp.zeros((ROWS, 128), BF16)


def pick_kernel(
    where_ref, ids_ref, middle_ref, f0, f1, f2a, f2b, f3, out_ref, other_ref
):
    y_index, c_index = where_ref[0], where_ref[1]
    owned = f0.shape[0]
    split = f2a.shape[0]
    middle_width = middle_ref.shape[2]
    zeros = jnp.zeros(f0.shape[1:], BF16)

    def step(z, carry):
        for core in range(C):
            for x in range(X):
                place = 4 * ((core + c_index) % C)
                fine_id = ids_ref[x, z, place + 1] * 32 + ids_ref[x, z, place + 2]
                owner = fine_id // owned
                choice = (y_index - owner // C + Y) % Y
                slot = fine_id % owned
                choice = jnp.where(owner % C == c_index, choice, Y + 1)
                choice = jnp.where(jnp.logical_and(choice == 2, slot >= split), Y, choice)
                rows = zeros
                for s, piece in enumerate((f0, f1, f2a, f3, f2b)):
                    here = choice == s
                    local = slot % split if s in (2, 4) else slot
                    rows = jnp.where(here, piece[local], rows)
                m = x * Z + z
                if core == 0:
                    out_ref[m, :, :middle_width] = middle_ref[ids_ref[x, z, place]]
                    out_ref[m, :, middle_width:] = rows
                else:
                    other_ref[m] = rows
        return carry

    lax.fori_loop(0, Z, step, 0, unroll=2)


def merge_kernel(send_ref, extra_ref, out_ref):
    middle_width = send_ref.shape[2] - extra_ref.shape[2]
    out_ref[:, :, :middle_width] = send_ref[:, :, :middle_width]
    out_ref[:, :, middle_width:] = send_ref[:, :, middle_width:] + extra_ref[...]


def coarse_kernel(
    where_ref, ids_ref, x_ref, g_ref, ox_ref, og_ref, h0, h1, h2a, h2b, h3,
    s0, s1, s2, s3, back_ref, other_back_ref, half_ref, own_term, other_term,
):
    y_index = where_ref[0]
    c_index, x_index, z_index = where_ref[1], where_ref[2], where_ref[3]
    own_id = ids_ref[x_index, z_index, 4 * c_index] // 16
    other_id = ids_ref[x_index, z_index, 4 * (1 - c_index)] // 16
    width = h0.shape[1] // 2

    def level(identity, inputs, upstream, term_ref, into_ref):
        choice = (y_index - identity + Y) % Y
        for s, ref in ((0, h0), (1, h1), (3, h3)):

            @pl.when(choice == s)
            def _(ref=ref):
                half_ref[...] = ref[...]

        @pl.when(choice == 2)
        def _():
            half_ref[: h2a.shape[0]] = h2a[...]
            half_ref[h2a.shape[0] :] = h2b[...]

        tokens, cotangent = inputs[...], upstream[...]
        before = dot(tokens, half_ref[:, :width], 1, 0)
        hidden_grad = dot(cotangent, half_ref[:, width:], 1, 0)
        hidden, before_grad = gelu_pair(before, hidden_grad)
        term_ref[:, :width] = dot(tokens, before_grad, 0, 0)
        term_ref[:, width:] = dot(cotangent, hidden, 0, 0)
        into_ref[...] = dot(before_grad, half_ref[:, :width], 1, 1)

    level(own_id, x_ref, g_ref, own_term, back_ref)
    level(other_id, ox_ref, og_ref, other_term, other_back_ref)
    for s, ref in enumerate((s0, s1, s2, s3)):
        block = (y_index + s) % Y
        own, other = own_id == block, other_id == block

        @pl.when(jnp.logical_and(own, other))
        def _(ref=ref):
            ref[...] = (own_term[...] + other_term[...]).astype(BF16)

        @pl.when(jnp.logical_and(own, jnp.logical_not(other)))
        def _(ref=ref):
            ref[...] = own_term[...].astype(BF16)

        @pl.when(jnp.logical_and(other, jnp.logical_not(own)))
        def _(ref=ref):
            ref[...] = other_term[...].astype(BF16)

        @pl.when(jnp.logical_not(jnp.logical_or(own, other)))
        def _(ref=ref):
            ref[...] = jnp.zeros(ref.shape, BF16)


def levels_kernel(x_ref, g_ref, w_ref, term_ref, back_ref):
    tokens, cotangent = x_ref[...], g_ref[...]
    middle = 256
    half = middle // 2
    before = dot(tokens, w_ref[:, :half], 1, 0)
    hidden_grad = dot(cotangent, w_ref[:, half:middle], 1, 0)
    hidden, before_grad = gelu_pair(before, hidden_grad)
    fine = w_ref[:, middle:]
    width = fine.shape[1]
    fine_before = dot(tokens, fine, 1, 0)
    fine_hidden_grad = pltpu.roll(dot(cotangent, fine, 1, 0), width // 2, 1)
    first = lax.broadcasted_iota(I32, fine_before.shape, 1) < width // 2
    fine_before = jnp.where(first, fine_before, 0.0)
    fine_hidden_grad = jnp.where(first, fine_hidden_grad, 0.0)
    fine_hidden, fine_before_grad = gelu_pair(fine_before, fine_hidden_grad)
    fine_hidden = pltpu.roll(fine_hidden.astype(F32), width // 2, 1).astype(BF16)
    term_ref[:, :half] = dot(tokens, before_grad, 0, 0).astype(BF16)
    term_ref[:, half:middle] = dot(cotangent, hidden, 0, 0).astype(BF16)
    term_ref[:, middle:] = (
        dot(tokens, fine_before_grad, 0, 0) + dot(cotangent, fine_hidden, 0, 0)
    ).astype(BF16)
    back_ref[...] = dot(before_grad, w_ref[:, :half], 1, 1) + dot(fine_before_grad, fine, 1, 1)


def collect_kernel(where_ref, ids_ref, parts_ref, keep_ref, leave_ref, sums_ref):
    c_index = where_ref[1]
    middle = keep_ref.shape[2]
    half = keep_ref.shape[0]
    share = half // Y
    sums_ref[...] = jnp.zeros(sums_ref.shape, F32)

    def step(z, carry):
        for x in range(X):
            block = ids_ref[x, z, 4 * c_index]
            owner = block // share
            side = (owner + c_index) % C
            place = side * half + (owner // C) * share + block % share
            m = x * Z + z
            sums_ref[place] = sums_ref[place] + parts_ref[m, :, :middle].astype(F32)
            pair = half + (x % (X // 2)) * Z + z
            low = (x // (X // 2)) * 128
            leave_ref[pair, :, low : low + 128] = parts_ref[m, :, middle:]
        return carry

    lax.fori_loop(0, Z, step, 0, unroll=2)
    keep_ref[...] = sums_ref[:half]
    leave_ref[:half] = sums_ref[half:].astype(BF16)


def combine_kernel(
    where_ref, keep_ref, leave_ref, arrived_ref, numbers_ref, packet_ref, s0, s1, s3
):
    y_index = where_ref[0]
    half = keep_ref.shape[0]
    share = half // Y
    pairs = MEMBERS // 2
    packet_ref[:pairs] = leave_ref[half:]
    packet_ref[pairs : 2 * pairs] = arrived_ref[half:]
    packet_ref[2 * pairs] = numbers_ref[0]
    for s, ref in ((0, s0), (1, s1), (3, s3)):
        at = pl.ds(((y_index + s) % Y) * share, share)
        ref[...] = keep_ref[at] + arrived_ref[at].astype(F32)
    at = pl.ds(((y_index + 2) % Y) * share, share)
    packet_ref[2 * pairs + 1 :] = (keep_ref[at] + arrived_ref[at].astype(F32)).astype(BF16)


def relay_kernel(r1, r3, s1, s3, up_ref, down_ref):
    pairs = MEMBERS // 2
    share = s1.shape[0]
    middle = 2 * pairs + 1
    split = share // 2
    up_ref[:pairs] = r1[:pairs]
    up_ref[pairs] = r1[2 * pairs]
    up_ref[pairs + 1 : pairs + 1 + split] = (
        s1[:split] + r1[middle : middle + split].astype(F32)
    ).astype(BF16)
    up_ref[pairs + 1 + split :] = s1[split:].astype(BF16)
    down_ref[:pairs] = r3[pairs : 2 * pairs]
    down_ref[pairs : pairs + split] = s3[:split].astype(BF16)
    down_ref[pairs + split :] = (s3[split:] + r3[middle + split :].astype(F32)).astype(BF16)


def add_fine(group, c_index, owned, ids_ref, p, core, piece, base, sums_ref):
    def step(z, carry):
        for x in range(X):
            place = x * 8 + 4 * ((core + c_index) % C)
            fine_id = ids_ref[p, z, place + 1] * 32 + ids_ref[p, z, place + 2]
            slot = jnp.where(fine_id // owned == group, fine_id % owned, owned)
            pair = base + (x % (X // 2)) * Z + z
            low = (x // (X // 2)) * 128
            part = piece[pair, :, low : low + 128]
            sums_ref[slot] = sums_ref[slot] + part.astype(F32)
        return carry

    lax.fori_loop(0, Z, step, 0, unroll=4)


def first_fine_kernel(where_ref, ids_ref, p0, p1, p3, sums_ref):
    group = where_ref[0] * C + where_ref[1]
    owned = sums_ref.shape[0] - 8
    sums_ref[...] = jnp.zeros(sums_ref.shape, F32)
    for p, piece in enumerate((p0, p1, p3)):
        for core in range(C):
            base = core * (MEMBERS // 2)
            add_fine(group, where_ref[1], owned, ids_ref, p, core, piece, base, sums_ref)


def last_fine_kernel(where_ref, ids_ref, before_ref, q1, q3, out_ref, sums_ref):
    group = where_ref[0] * C + where_ref[1]
    owned = sums_ref.shape[0] - 8
    sums_ref[...] = before_ref[...]
    for core, piece in enumerate((q1, q3)):
        add_fine(group, where_ref[1], owned, ids_ref, 0, core, piece, 0, sums_ref)
    out_ref[...] = sums_ref[:owned].astype(BF16)


def spread_kernel(total_ref, coarse_ref, middle_ref):
    share = total_ref.shape[1] - 1
    width = total_ref.shape[3] // 2
    for y in range(Y):
        for core in range(C):
            g = y * C + core
            middle_ref[g * share : (g + 1) * share] = total_ref[g, :share]
            low = core * width
            coarse_ref[y, :, low : low + width] = total_ref[g, share, :, :width]
            low = (C + core) * width
            coarse_ref[y, :, low : low + width] = total_ref[g, share, :, width:]


def on_device(tokens, cotangent, path, coarse_weights, middle_weights, fine_weights):
    y_index, c_index = lax.axis_index("y"), lax.axis_index("c")
    x_index = lax.axis_index("x")
    where = jnp.stack([y_index, c_index, x_index, lax.axis_index("z")]).astype(I32)
    fine_owned, _, fine_width = fine_weights.shape
    coarse_width = coarse_weights.shape[2]
    middle_width = middle_weights.shape[2]
    half = coarse_width // 2
    depth = MEMBERS * ROWS

    other_path = shift(path, "c", 1)
    packet = kernel_call(packet_kernel, [SMEM, SMEM, SMEM, VMEM], bf16(Z, ROWS, half + 128))(
        where, path, other_path, coarse_weights
    )
    packets = gather(exchange(packet, "z"), "x").reshape(X, Z, ROWS, half + 128)

    fine_one = shift(after(fine_weights, packet), "y", 1)
    fine_three = shift(after(fine_weights, packet), "y", 3)
    split = fine_owned // 2
    fine_rows = [
        fine_weights,
        fine_one,
        shift(fine_one[:split], "y", 1),
        shift(fine_three[split:], "y", 3),
        fine_three,
    ]
    both = jnp.concatenate([after(tokens, packet), cotangent], axis=0)
    other_both = shift(both, "c", 1)
    *fine_rows, other_both = lax.optimization_barrier(fine_rows + [other_both])

    ids = packets[:, :, 0, half : half + 4 * C].astype(I32)
    send, extra = kernel_call(
        pick_kernel,
        [SMEM, SMEM, VMEM] + [VMEM] * 5,
        (bf16(MEMBERS, ROWS, middle_width + fine_width), bf16(MEMBERS, ROWS, fine_width)),
    )(where, ids, middle_weights, *fine_rows)
    send = kernel_call(merge_kernel, [VMEM] * 2, bf16(*send.shape))(send, shift(extra, "c", 1))
    mine = exchange(send, ("x", "z")).reshape(depth, -1)

    numbers = kernel_call(numbers_kernel, [VMEM], bf16(1, ROWS, 2 * fine_width))(
        after(packets, send)
    )
    block = after(packets, send)[:, :, :, :half].reshape(depth, half)
    one, three = shift(block, "y", 1), shift(block, "y", 3)
    middle_row = depth // 2
    halves = [
        block,
        one,
        shift(one[:middle_row], "y", 1),
        shift(three[middle_row:], "y", 3),
        three,
    ]
    length = tokens.shape[0]
    slots = kernel_call(
        coarse_kernel,
        [SMEM, SMEM] + [VMEM] * 9,
        tuple([bf16(depth, half)] * Y + [f32(length, depth)] * 2),
        [
            pltpu.VMEM((depth, half), BF16),
            pltpu.VMEM((depth, half), F32),
            pltpu.VMEM((depth, half), F32),
        ],
        cost=10_000_000,
    )(
        where, ids, tokens, cotangent, other_both[:length], other_both[length:], *halves
    )
    mine, numbers, *slots = lax.optimization_barrier([mine, numbers] + list(slots))
    slots, coarse_back, other_back = slots[:Y], slots[Y], slots[Y + 1]

    terms, back = kernel_call(
        levels_kernel,
        [VMEM] * 3,
        (bf16(depth, middle_width + fine_width), f32(length, depth)),
        cost=10_000_000,
    )(tokens, cotangent, mine)
    parts = exchange(terms.reshape(MEMBERS, ROWS, -1), ("x", "z"))

    up = shift(slots[2][:middle_row], "y", 1).astype(F32)
    down = shift(slots[2][middle_row:], "y", 3).astype(F32)
    up = (slots[1][:middle_row].astype(F32) + up).astype(BF16)
    down = (slots[3][middle_row:].astype(F32) + down).astype(BF16)
    up = shift(jnp.concatenate([up, slots[1][middle_row:]]), "y", 1).astype(F32)
    down = shift(jnp.concatenate([slots[3][:middle_row], down]), "y", 3).astype(F32)
    summed = (slots[0].astype(F32) + up + down).astype(BF16).reshape(X, Z * ROWS, half)
    column_sum = lax.dynamic_index_in_dim(summed, x_index, 0, keepdims=False).astype(F32)
    for s in range(1, X):
        leaving = lax.dynamic_index_in_dim(summed, (x_index + s) % X, 0, keepdims=False)
        column_sum = column_sum + shift(leaving, "x", s).astype(F32)
    column_sum = column_sum.astype(BF16).reshape(Z, ROWS, half)
    parts, column_sum = lax.optimization_barrier((parts, column_sum))
    coarse_four = exchange(column_sum, "z")

    middle_count = middle_weights.shape[0]
    pairs = MEMBERS // 2
    side = middle_count // C
    share = side // Y
    keep, leave = kernel_call(
        collect_kernel,
        [SMEM, SMEM, VMEM],
        (f32(side, ROWS, middle_width), bf16(side + pairs, ROWS, middle_width)),
        [pltpu.VMEM((middle_count, ROWS, middle_width), F32)],
    )(where, ids, parts)
    arrived = shift(leave, "c", 1)
    first, s0, s1, s3 = kernel_call(
        combine_kernel,
        [SMEM] + [VMEM] * 4,
        tuple([bf16(2 * pairs + 1 + share, ROWS, middle_width)] + [f32(share, ROWS, middle_width)] * 3),
    )(where, keep, leave, arrived, numbers)
    r1, r3 = shift(first, "y", 1), shift(first, "y", 3)
    second = kernel_call(
        relay_kernel,
        [VMEM] * 4,
        (
            bf16(pairs + 1 + share, ROWS, middle_width),
            bf16(pairs + share, ROWS, middle_width),
        ),
    )(r1, r3, s1, s3)
    q1, q3 = shift(second[0], "y", 1), shift(second[1], "y", 3)
    fine_ids = [f[2 * pairs, :Z, : 4 * C * X].astype(I32) for f in (first, r1, r3)]
    fine_sums = kernel_call(
        first_fine_kernel,
        [SMEM, SMEM] + [VMEM] * 3,
        f32(fine_owned + 8, ROWS, fine_width),
    )(where, jnp.stack(fine_ids), first, r1, r3)
    fine_sums, q1, q3 = lax.optimization_barrier((fine_sums, q1, q3))
    other_back = shift(after(other_back, second[0]), "c", 1)
    tokens_grad = (coarse_back + other_back + back).astype(BF16)
    middle_done = s0 + q1[pairs + 1 :].astype(F32) + q3[pairs:].astype(F32)
    coarse_four, middle_done = lax.optimization_barrier((coarse_four, middle_done))
    coarse_done = jnp.sum(coarse_four, axis=0, dtype=F32).astype(BF16)
    done = jnp.concatenate([middle_done.astype(BF16), coarse_done[None]], axis=0)
    total = gather(done, ("y", "c")).reshape((Y * C,) + done.shape)
    coarse_total, middle_total = kernel_call(
        spread_kernel, [VMEM], (bf16(*coarse_weights.shape), bf16(*middle_weights.shape))
    )(total)
    fine_total = kernel_call(
        last_fine_kernel,
        [SMEM, SMEM] + [VMEM] * 3,
        bf16(fine_owned, ROWS, fine_width),
        [pltpu.VMEM((fine_owned + 8, ROWS, fine_width), F32)],
    )(where, q1[pairs, :Z, : 4 * C * X].astype(I32)[None], fine_sums, q1, q3)
    return (tokens_grad, coarse_total, middle_total, fine_total)


def solution(mesh):
    fine_mesh = Mesh(mesh.devices.reshape(Y, C, X, Z), EVERYONE)
    members = ("x", "z")
    return jax.shard_map(
        on_device,
        mesh=fine_mesh,
        in_specs=(
            P(EVERYONE, None),
            P(EVERYONE, None),
            P(EVERYONE, None),
            P(None, members, None),
            P(None, members, None),
            P(("y", "c"), members, None),
        ),
        out_specs=(
            P(EVERYONE, None),
            P(None, members, None),
            P(None, members, None),
            P(("y", "c"), members, None),
        ),
        check_vma=False,
    )
```

```python
from functools import partial

import jax
import jax.numpy as jnp
from jax import lax
from jax.experimental import pallas as pl
from jax.experimental.pallas import tpu as pltpu
from jax.sharding import Mesh, PartitionSpec as P

F32 = jnp.float32
BF16 = jnp.bfloat16
I32 = jnp.int32
Y, C, X, Z = 4, 2, 4, 16
MEMBERS = X * Z
ROWS = 16
LANES = 8
EVERYONE = ("y", "c", "x", "z")
VMEM = pl.BlockSpec(memory_space=pltpu.VMEM)
SMEM = pl.BlockSpec(memory_space=pltpu.SMEM)


def exchange(array, axes):
    return lax.all_to_all(array, axes, split_axis=0, concat_axis=0, tiled=True)


def gather(array, axes):
    count = lax.axis_size(axes)
    return exchange(jnp.broadcast_to(array[None], (count,) + array.shape), axes)


def shift(array, axis, step):
    count = lax.axis_size(axis)
    return lax.ppermute(array, axis, [(i, (i + step) % count) for i in range(count)])


def after(array, *others):
    return lax.optimization_barrier((array,) + others)[0]


def kernel_call(body, in_specs, out_shape, scratch=(), cost=1_000_000, limit=16):
    return pl.pallas_call(
        body,
        out_shape=out_shape,
        in_specs=in_specs,
        out_specs=jax.tree.map(lambda _: VMEM, out_shape),
        scratch_shapes=list(scratch),
        compiler_params=pltpu.CompilerParams(vmem_limit_bytes=limit * 1024 * 1024),
        cost_estimate=pl.CostEstimate(flops=cost, bytes_accessed=cost, transcendentals=0),
    )


def bf16(*shape):
    return jax.ShapeDtypeStruct(shape, BF16)


def f32(*shape):
    return jax.ShapeDtypeStruct(shape, F32)


def dot(left, right, left_dim, right_dim):
    return lax.dot_general(
        left, right, (((left_dim,), (right_dim,)), ((), ())), preferred_element_type=F32
    )


def gelu_pair(v, upstream):
    scale = 0.7978845608028654
    square = v * v
    t = jnp.tanh(scale * (v + 0.044715 * (square * v)))
    half = 0.5 * (1.0 + t)
    slope = half + 0.5 * v * (1.0 - t * t) * (scale * (1.0 + 0.134145 * square))
    return (v * half).astype(BF16), (upstream * slope).astype(BF16)


def packet_kernel(owned, where_ref, own_ref, other_ref, coarse_ref, out_ref):
    y_index, c_index = where_ref[0], where_ref[1]
    width = coarse_ref.shape[2] // 4
    up = coarse_ref[y_index, :, pl.ds(pl.multiple_of(c_index * width, width), width)]
    down = coarse_ref[
        y_index, :, pl.ds(pl.multiple_of((c_index + 2) * width, width), width)
    ]
    lanes = lax.broadcasted_iota(I32, (ROWS, 128), 1)
    numbers = jnp.zeros((ROWS, 128), F32)
    for core, ref in ((c_index, own_ref), (1 - c_index, other_ref)):
        fine_id = ref[0, 2]
        owner, slot = fine_id // owned, fine_id % owned
        choice = (y_index - owner // C + Y) % Y
        choice = jnp.where(jnp.logical_and(choice == 2, slot >= owned // 2), Y, choice)
        choice = jnp.where(owner % C == c_index, choice, Y + 1)
        code = choice * owned + slot
        values = (ref[0, 1], fine_id // 32, fine_id % 32, code // 32, code % 32)
        for i, value in enumerate(values):
            numbers = jnp.where(lanes == LANES * core + i, value.astype(F32), numbers)
    numbers = numbers.astype(BF16)
    for z in range(Z):
        out_ref[z, :, :width] = up
        out_ref[z, :, width : 2 * width] = down
        out_ref[z, :, 2 * width :] = numbers


def numbers_kernel(grid_ref, out_ref):
    width = grid_ref.shape[3] - 128
    rows = lax.broadcasted_iota(I32, (ROWS, 128), 0)
    total = jnp.zeros((ROWS, 128), F32)
    for x in range(X):
        line = jnp.zeros((ROWS, 128), F32)
        for z in range(Z):
            line = jnp.where(rows == z, grid_ref[x, z, :, width:].astype(F32), line)
        total = total + (pltpu.roll(line, LANES * C * x, 1) if x else line)
    out_ref[0, :, :128] = total.astype(BF16)
    out_ref[0, :, 128:] = jnp.zeros((ROWS, 128), BF16)


def chosen(code, pieces):
    owned = pieces[0].shape[0]
    choice, local = code // owned, code % owned
    rows = jnp.zeros(pieces[0].shape[1:], BF16)
    for s, piece in enumerate(pieces):
        at = local if piece.shape[0] == owned else local % piece.shape[0]
        rows = jnp.where(choice == s, piece[at], rows)
    return rows


def code_of(ids_ref, x, z, core):
    return ids_ref[x, z, LANES * core + 3] * 32 + ids_ref[x, z, LANES * core + 4]


def pick_other_kernel(where_ref, ids_ref, f0, f1, f2a, f3, f2b, out_ref):
    core = 1 - where_ref[1]

    def step(z, carry):
        for x in range(X):
            code = code_of(ids_ref, x, z, core)
            out_ref[x * Z + z] = chosen(code, (f0, f1, f2a, f3, f2b))
        return carry

    lax.fori_loop(0, Z, step, 0, unroll=4)


def pick_own_kernel(where_ref, ids_ref, middle_ref, f0, f1, f2a, f3, f2b, out_ref):
    core = where_ref[1]
    middle_width = middle_ref.shape[2]

    def step(z, carry):
        for x in range(X):
            m = x * Z + z
            code = code_of(ids_ref, x, z, core)
            out_ref[m, :, :middle_width] = middle_ref[ids_ref[x, z, LANES * core]]
            out_ref[m, :, middle_width:] = chosen(code, (f0, f1, f2a, f3, f2b))
        return carry

    lax.fori_loop(0, Z, step, 0, unroll=4)


def merge_kernel(send_ref, extra_ref, out_ref):
    middle_width = send_ref.shape[2] - extra_ref.shape[2]
    out_ref[:, :, :middle_width] = send_ref[:, :, :middle_width]
    out_ref[:, :, middle_width:] = send_ref[:, :, middle_width:] + extra_ref[...]


def coarse_kernel(
    where_ref, ids_ref, x_ref, g_ref, ox_ref, og_ref, h0, h1, h2a, h2b, h3,
    s0, s1, s2, s3, back_ref, other_back_ref, half_ref, own_term, other_term,
):
    y_index = where_ref[0]
    c_index, x_index, z_index = where_ref[1], where_ref[2], where_ref[3]
    own_id = ids_ref[x_index, z_index, LANES * c_index] // 16
    other_id = ids_ref[x_index, z_index, LANES * (1 - c_index)] // 16
    width = h0.shape[1] // 2

    def level(identity, inputs, upstream, term_ref, into_ref):
        choice = (y_index - identity + Y) % Y
        for s, ref in ((0, h0), (1, h1), (3, h3)):

            @pl.when(choice == s)
            def _(ref=ref):
                half_ref[...] = ref[...]

        @pl.when(choice == 2)
        def _():
            half_ref[: h2a.shape[0]] = h2a[...]
            half_ref[h2a.shape[0] :] = h2b[...]

        tokens, cotangent = inputs[...], upstream[...]
        before = dot(tokens, half_ref[:, :width], 1, 0)
        hidden_grad = dot(cotangent, half_ref[:, width:], 1, 0)
        hidden, before_grad = gelu_pair(before, hidden_grad)
        term_ref[:, :width] = dot(tokens, before_grad, 0, 0)
        term_ref[:, width:] = dot(cotangent, hidden, 0, 0)
        into_ref[...] = dot(before_grad, half_ref[:, :width], 1, 1)

    level(own_id, x_ref, g_ref, own_term, back_ref)
    level(other_id, ox_ref, og_ref, other_term, other_back_ref)
    for s, ref in enumerate((s0, s1, s2, s3)):
        block = (y_index + s) % Y
        own, other = own_id == block, other_id == block

        @pl.when(jnp.logical_and(own, other))
        def _(ref=ref):
            ref[...] = (own_term[...] + other_term[...]).astype(BF16)

        @pl.when(jnp.logical_and(own, jnp.logical_not(other)))
        def _(ref=ref):
            ref[...] = own_term[...].astype(BF16)

        @pl.when(jnp.logical_and(other, jnp.logical_not(own)))
        def _(ref=ref):
            ref[...] = other_term[...].astype(BF16)

        @pl.when(jnp.logical_not(jnp.logical_or(own, other)))
        def _(ref=ref):
            ref[...] = jnp.zeros(ref.shape, BF16)


def levels_kernel(x_ref, g_ref, w_ref, term_ref, back_ref):
    tokens, cotangent = x_ref[...], g_ref[...]
    middle = 256
    half = middle // 2
    before = dot(tokens, w_ref[:, :half], 1, 0)
    hidden_grad = dot(cotangent, w_ref[:, half:middle], 1, 0)
    hidden, before_grad = gelu_pair(before, hidden_grad)
    fine = w_ref[:, middle:]
    width = fine.shape[1]
    fine_before = dot(tokens, fine, 1, 0)
    fine_hidden_grad = pltpu.roll(dot(cotangent, fine, 1, 0), width // 2, 1)
    first = lax.broadcasted_iota(I32, fine_before.shape, 1) < width // 2
    fine_before = jnp.where(first, fine_before, 0.0)
    fine_hidden_grad = jnp.where(first, fine_hidden_grad, 0.0)
    fine_hidden, fine_before_grad = gelu_pair(fine_before, fine_hidden_grad)
    fine_hidden = pltpu.roll(fine_hidden.astype(F32), width // 2, 1).astype(BF16)
    term_ref[:, :half] = dot(tokens, before_grad, 0, 0).astype(BF16)
    term_ref[:, half:middle] = dot(cotangent, hidden, 0, 0).astype(BF16)
    term_ref[:, middle:] = (
        dot(tokens, fine_before_grad, 0, 0) + dot(cotangent, fine_hidden, 0, 0)
    ).astype(BF16)
    back_ref[...] = dot(before_grad, w_ref[:, :half], 1, 1) + dot(fine_before_grad, fine, 1, 1)


def collect_kernel(
    where_ref, ids_ref, numbers_ref, parts_ref, packet_ref, s0, s1, s3, sums_ref
):
    y_index, c_index = where_ref[0], where_ref[1]
    middle = parts_ref.shape[2] - 128
    slot = s0.shape[0]
    pairs = MEMBERS // 2
    sums_ref[...] = jnp.zeros(sums_ref.shape, F32)

    def step(zz, carry):
        for x in range(X):
            for h in range(2):
                z = 2 * zz + h
                block = ids_ref[x, z, LANES * c_index]
                place = ((block // slot - y_index + Y) % Y) * slot + block % slot
                m = x * Z + z
                sums_ref[place] = sums_ref[place] + parts_ref[m, :, :middle].astype(F32)
                pair = x * (Z // 2) + zz
                packet_ref[pair, :, h * 128 : h * 128 + 128] = parts_ref[m, :, middle:]
        return carry

    lax.fori_loop(0, Z // 2, step, 0)
    packet_ref[pairs] = numbers_ref[0]
    packet_ref[pairs + 1 :] = sums_ref[2 * slot : 3 * slot].astype(BF16)
    s0[...] = sums_ref[:slot]
    s1[...] = sums_ref[slot : 2 * slot]
    s3[...] = sums_ref[3 * slot :]


def relay_kernel(r1, r3, s1, s3, up_ref, down_ref):
    pairs = MEMBERS // 2
    lower = pairs // 2
    split = s1.shape[0] // 2
    middle = pairs + 1
    up_ref[:lower] = r1[:lower]
    up_ref[lower] = r1[pairs]
    up_ref[lower + 1 : lower + 1 + split] = (
        s1[:split] + r1[middle : middle + split].astype(F32)
    ).astype(BF16)
    up_ref[lower + 1 + split :] = s1[split:].astype(BF16)
    down_ref[:lower] = r3[lower:pairs]
    down_ref[lower : lower + split] = s3[:split].astype(BF16)
    down_ref[lower + split :] = (s3[split:] + r3[middle + split :].astype(F32)).astype(BF16)


def add_fine(where_ref, owned, ids_ref, p, piece, xs, sums_ref):
    y_index, c_index = where_ref[0], where_ref[1]

    def step(zz, carry):
        for x in xs:
            for h in range(2):
                place = LANES * (C * x + c_index)
                z = 2 * zz + h
                fine_id = ids_ref[p, z, place + 1] * 32 + ids_ref[p, z, place + 2]
                owner = fine_id // owned
                slot = ((owner + c_index) % C) * owned + fine_id % owned
                slot = jnp.where(owner // C == y_index, slot, C * owned)
                pair = (x - xs[0]) * (Z // 2) + zz
                part = piece[pair, :, h * 128 : h * 128 + 128]
                sums_ref[slot] = sums_ref[slot] + part.astype(F32)
        return carry

    lax.fori_loop(0, Z // 2, step, 0)


def first_fine_kernel(where_ref, ids_ref, p0, p1, p3, sums_ref):
    owned = (sums_ref.shape[0] - 8) // C
    sums_ref[...] = jnp.zeros(sums_ref.shape, F32)
    for p, piece in enumerate((p0, p1, p3)):
        add_fine(where_ref, owned, ids_ref, p, piece, range(X), sums_ref)


def last_fine_kernel(
    where_ref, ids_ref, before_ref, s0, q1, q3, leave_ref, middle_ref, fine_ref, sums_ref
):
    owned = fine_ref.shape[0]
    share = middle_ref.shape[0]
    lower = MEMBERS // 4
    sums_ref[...] = before_ref[...]
    add_fine(where_ref, owned, ids_ref, 0, q1, range(X // 2), sums_ref)
    add_fine(where_ref, owned, ids_ref, 0, q3, range(X // 2, X), sums_ref)
    fine_ref[...] = sums_ref[:owned]
    half = owned // 2
    leave_ref[share:, :, :128] = sums_ref[owned : owned + half].astype(BF16)
    leave_ref[share:, :, 128:] = sums_ref[owned + half : 2 * owned].astype(BF16)

    def middle_of(side):
        low = side * share
        return (
            s0[pl.ds(low, share)]
            + q1[pl.ds(lower + 1 + low, share)].astype(F32)
            + q3[pl.ds(lower + low, share)].astype(F32)
        )

    middle_ref[...] = middle_of(where_ref[1])
    leave_ref[:share] = middle_of(1 - where_ref[1]).astype(BF16)


def finish_kernel(fine_ref, arrived_ref, out_ref):
    half = fine_ref.shape[0] // 2
    share = arrived_ref.shape[0] - half
    for h in range(2):
        low = h * half
        out_ref[low : low + half] = (
            fine_ref[low : low + half]
            + arrived_ref[share:, :, h * 128 : h * 128 + 128].astype(F32)
        ).astype(BF16)


def spread_kernel(total_ref, coarse_ref, middle_ref):
    share = total_ref.shape[1] - 1
    width = total_ref.shape[3] // 2
    for y in range(Y):
        for core in range(C):
            g = y * C + core
            middle_ref[g * share : (g + 1) * share] = total_ref[g, :share]
            low = core * width
            coarse_ref[y, :, low : low + width] = total_ref[g, share, :, :width]
            low = (C + core) * width
            coarse_ref[y, :, low : low + width] = total_ref[g, share, :, width:]


def on_device(tokens, cotangent, path, coarse_weights, middle_weights, fine_weights):
    y_index, c_index = lax.axis_index("y"), lax.axis_index("c")
    x_index = lax.axis_index("x")
    where = jnp.stack([y_index, c_index, x_index, lax.axis_index("z")]).astype(I32)
    fine_owned, _, fine_width = fine_weights.shape
    coarse_width = coarse_weights.shape[2]
    middle_width = middle_weights.shape[2]
    half = coarse_width // 2
    depth = MEMBERS * ROWS

    other_path = shift(path, "c", 1)
    packet = kernel_call(
        partial(packet_kernel, fine_owned),
        [SMEM, SMEM, SMEM, VMEM],
        bf16(Z, ROWS, half + 128),
    )(where, path, other_path, coarse_weights)
    packets = exchange(packet, "z")

    fine_one = shift(after(fine_weights, packet), "y", 1)
    fine_three = shift(after(fine_weights, packet), "y", 3)
    packets, fine_one, fine_three = lax.optimization_barrier((packets, fine_one, fine_three))
    packets = gather(packets, "x").reshape(X, Z, ROWS, half + 128)
    split = fine_owned // 2
    fine_rows = [
        fine_weights,
        fine_one,
        shift(fine_one[:split], "y", 1),
        fine_three,
        shift(fine_three[split:], "y", 3),
    ]
    ids = packets[:, :, 0, half : half + LANES * C].astype(I32)
    extra = kernel_call(
        pick_other_kernel, [SMEM] * 2 + [VMEM] * 5, bf16(MEMBERS, ROWS, fine_width)
    )(where, ids, *fine_rows)
    arrived = shift(extra, "c", 1)
    send = kernel_call(
        pick_own_kernel,
        [SMEM] * 2 + [VMEM] * 6,
        bf16(MEMBERS, ROWS, middle_width + fine_width),
    )(where, ids, middle_weights, *fine_rows)
    send = kernel_call(merge_kernel, [VMEM] * 2, bf16(*send.shape))(send, arrived)
    mine = exchange(send, ("x", "z")).reshape(depth, -1)

    both = jnp.concatenate([after(tokens, send), cotangent], axis=0)
    other_both = shift(both, "c", 1)

    numbers = kernel_call(numbers_kernel, [VMEM], bf16(1, ROWS, 2 * fine_width))(
        after(packets, send)
    )
    block = after(packets, send)[:, :, :, :half].reshape(depth, half)
    one, three = shift(block, "y", 1), shift(block, "y", 3)
    middle_row = depth // 2
    halves = [
        block,
        one,
        shift(one[:middle_row], "y", 1),
        shift(three[middle_row:], "y", 3),
        three,
    ]
    length = tokens.shape[0]
    slots = kernel_call(
        coarse_kernel,
        [SMEM, SMEM] + [VMEM] * 9,
        tuple([bf16(depth, half)] * Y + [f32(length, depth)] * 2),
        [
            pltpu.VMEM((depth, half), BF16),
            pltpu.VMEM((depth, half), F32),
            pltpu.VMEM((depth, half), F32),
        ],
        cost=10_000_000,
    )(
        where, ids, tokens, cotangent, other_both[:length], other_both[length:], *halves
    )
    mine, numbers, *slots = lax.optimization_barrier([mine, numbers] + list(slots))
    slots, coarse_back, other_back = slots[:Y], slots[Y], slots[Y + 1]

    terms, back = kernel_call(
        levels_kernel,
        [VMEM] * 3,
        (bf16(depth, middle_width + fine_width), f32(length, depth)),
        cost=10_000_000,
    )(tokens, cotangent, mine)
    parts = exchange(terms.reshape(MEMBERS, ROWS, -1), ("x", "z"))

    up = shift(slots[2][:middle_row], "y", 1).astype(F32)
    down = shift(slots[2][middle_row:], "y", 3).astype(F32)
    up = (slots[1][:middle_row].astype(F32) + up).astype(BF16)
    down = (slots[3][middle_row:].astype(F32) + down).astype(BF16)
    up = shift(jnp.concatenate([up, slots[1][middle_row:]]), "y", 1).astype(F32)
    down = shift(jnp.concatenate([slots[3][:middle_row], down]), "y", 3).astype(F32)
    summed = (slots[0].astype(F32) + up + down).astype(BF16).reshape(X, Z * ROWS, half)
    column_sum = lax.dynamic_index_in_dim(summed, x_index, 0, keepdims=False).astype(F32)
    for s in range(1, X):
        leaving = lax.dynamic_index_in_dim(summed, (x_index + s) % X, 0, keepdims=False)
        column_sum = column_sum + shift(leaving, "x", s).astype(F32)
    column_sum = column_sum.astype(BF16).reshape(Z, ROWS, half)
    parts, column_sum = lax.optimization_barrier((parts, column_sum))

    middle_count = middle_weights.shape[0]
    pairs = MEMBERS // 2
    lower = pairs // 2
    quarter_count = middle_count // Y
    share = quarter_count // C
    first, s0, s1, s3 = kernel_call(
        collect_kernel,
        [SMEM, SMEM, VMEM, VMEM],
        tuple(
            [bf16(pairs + 1 + quarter_count, ROWS, middle_width)]
            + [f32(quarter_count, ROWS, middle_width)] * 3
        ),
        [pltpu.VMEM((middle_count, ROWS, middle_width), F32)],
    )(where, ids, numbers, parts)
    r1, r3 = shift(first, "y", 1), shift(first, "y", 3)
    coarse_four = exchange(after(column_sum, first), "z")
    second = kernel_call(
        relay_kernel,
        [VMEM] * 4,
        (
            bf16(lower + 1 + quarter_count, ROWS, middle_width),
            bf16(lower + quarter_count, ROWS, middle_width),
        ),
    )(r1, r3, s1, s3)
    q1, q3 = shift(second[0], "y", 1), shift(second[1], "y", 3)
    fine_ids = [f[pairs, :Z, : LANES * C * X].astype(I32) for f in (first, r1, r3)]
    fine_sums = kernel_call(
        first_fine_kernel,
        [SMEM, SMEM] + [VMEM] * 3,
        f32(C * fine_owned + 8, ROWS, fine_width),
    )(where, jnp.stack(fine_ids), first, r1, r3)
    fine_sums, q1, q3, coarse_four = lax.optimization_barrier(
        (fine_sums, q1, q3, coarse_four)
    )
    leave, middle_done, fine_kept = kernel_call(
        last_fine_kernel,
        [SMEM, SMEM] + [VMEM] * 4,
        (
            bf16(share + fine_owned // 2, ROWS, middle_width),
            f32(share, ROWS, middle_width),
            f32(fine_owned, ROWS, fine_width),
        ),
        [pltpu.VMEM((C * fine_owned + 8, ROWS, fine_width), F32)],
    )(where, q1[lower, :Z, : LANES * C * X].astype(I32)[None], fine_sums, s0, q1, q3)
    arrived = shift(leave, "c", 1)
    coarse_done = jnp.sum(coarse_four, axis=0, dtype=F32).astype(BF16)
    middle_done = (middle_done + arrived[:share].astype(F32)).astype(BF16)
    done = jnp.concatenate([middle_done, coarse_done[None]], axis=0)
    total = gather(done, ("y", "c")).reshape((Y * C,) + done.shape)
    coarse_total, middle_total = kernel_call(
        spread_kernel, [VMEM], (bf16(*coarse_weights.shape), bf16(*middle_weights.shape))
    )(total)
    fine_total = kernel_call(
        finish_kernel, [VMEM] * 2, bf16(fine_owned, ROWS, fine_width)
    )(fine_kept, arrived)
    other_back = shift(after(other_back, second[0]), "c", 1)
    tokens_grad = (coarse_back + other_back + back).astype(BF16)
    return (tokens_grad, coarse_total, middle_total, fine_total)


def solution(mesh):
    fine_mesh = Mesh(mesh.devices.reshape(Y, C, X, Z), EVERYONE)
    members = ("x", "z")
    return jax.shard_map(
        on_device,
        mesh=fine_mesh,
        in_specs=(
            P(EVERYONE, None),
            P(EVERYONE, None),
            P(EVERYONE, None),
            P(None, members, None),
            P(None, members, None),
            P(("y", "c"), members, None),
        ),
        out_specs=(
            P(EVERYONE, None),
            P(None, members, None),
            P(None, members, None),
            P(("y", "c"), members, None),
        ),
        check_vma=False,
    )
```

```python
from functools import partial

import jax
import jax.numpy as jnp
from jax import lax
from jax.experimental import pallas as pl
from jax.experimental.pallas import tpu as pltpu
from jax.sharding import Mesh, PartitionSpec as P

F32 = jnp.float32
BF16 = jnp.bfloat16
I32 = jnp.int32
Y, C, X, Z = 4, 2, 4, 16
MEMBERS = X * Z
ROWS = 16
LANES = 8
EVERYONE = ("y", "c", "x", "z")
VMEM = pl.BlockSpec(memory_space=pltpu.VMEM)
SMEM = pl.BlockSpec(memory_space=pltpu.SMEM)


def exchange(array, axes):
    return lax.all_to_all(array, axes, split_axis=0, concat_axis=0, tiled=True)


def gather(array, axes):
    count = lax.axis_size(axes)
    return exchange(jnp.broadcast_to(array[None], (count,) + array.shape), axes)


def shift(array, axis, step):
    count = lax.axis_size(axis)
    return lax.ppermute(array, axis, [(i, (i + step) % count) for i in range(count)])


def after(array, *others):
    return lax.optimization_barrier((array,) + others)[0]


def kernel_call(body, in_specs, out_shape, scratch=(), cost=1_000_000, limit=16):
    return pl.pallas_call(
        body,
        out_shape=out_shape,
        in_specs=in_specs,
        out_specs=jax.tree.map(lambda _: VMEM, out_shape),
        scratch_shapes=list(scratch),
        compiler_params=pltpu.CompilerParams(vmem_limit_bytes=limit * 1024 * 1024),
        cost_estimate=pl.CostEstimate(flops=cost, bytes_accessed=cost, transcendentals=0),
    )


def bf16(*shape):
    return jax.ShapeDtypeStruct(shape, BF16)


def f32(*shape):
    return jax.ShapeDtypeStruct(shape, F32)


def dot(left, right, left_dim, right_dim):
    return lax.dot_general(
        left, right, (((left_dim,), (right_dim,)), ((), ())), preferred_element_type=F32
    )


def gelu_pair(v, upstream):
    scale = 0.7978845608028654
    square = v * v
    t = jnp.tanh(scale * (v + 0.044715 * (square * v)))
    half = 0.5 * (1.0 + t)
    slope = half + 0.5 * v * (1.0 - t * t) * (scale * (1.0 + 0.134145 * square))
    return (v * half).astype(BF16), (upstream * slope).astype(BF16)


def packet_kernel(owned, where_ref, own_ref, other_ref, coarse_ref, out_ref):
    y_index, c_index = where_ref[0], where_ref[1]
    width = coarse_ref.shape[2] // 4
    up = coarse_ref[y_index, :, pl.ds(pl.multiple_of(c_index * width, width), width)]
    down = coarse_ref[
        y_index, :, pl.ds(pl.multiple_of((c_index + 2) * width, width), width)
    ]
    lanes = lax.broadcasted_iota(I32, (ROWS, 128), 1)
    numbers = jnp.zeros((ROWS, 128), F32)
    for core, ref in ((c_index, own_ref), (1 - c_index, other_ref)):
        fine_id = ref[0, 2]
        owner, slot = fine_id // owned, fine_id % owned
        choice = (y_index - owner // C + Y) % Y
        choice = jnp.where(jnp.logical_and(choice == 2, slot >= owned // 2), Y, choice)
        choice = jnp.where(owner % C == c_index, choice, Y + 1)
        code = choice * owned + slot
        values = (ref[0, 1], fine_id // 32, fine_id % 32, code // 32, code % 32)
        for i, value in enumerate(values):
            numbers = jnp.where(lanes == LANES * core + i, value.astype(F32), numbers)
    numbers = numbers.astype(BF16)
    for z in range(Z):
        out_ref[z, :, :width] = up
        out_ref[z, :, width : 2 * width] = down
        out_ref[z, :, 2 * width :] = numbers


def repack_kernel(packets_ref, out_ref):
    width = out_ref.shape[2]
    rows = lax.broadcasted_iota(I32, (ROWS, 128), 0)
    line = jnp.zeros((ROWS, 128), F32)
    for z in range(Z):
        line = jnp.where(rows == z, packets_ref[z, :, width:].astype(F32), line)
    line = line.astype(BF16)
    for x in range(X):
        for z in range(Z):
            out_ref[x, z * ROWS : (z + 1) * ROWS] = packets_ref[z, :, :width]
        out_ref[x, Z * ROWS :, :128] = line
        out_ref[x, Z * ROWS :, 128:] = jnp.zeros((ROWS, width - 128), BF16)


def numbers_kernel(*refs):
    lines, out_ref = refs[:-1], refs[-1]
    total = jnp.zeros((ROWS, 128), F32)
    for x, ref in enumerate(lines):
        line = ref[:, :128].astype(F32)
        total = total + (pltpu.roll(line, LANES * C * x, 1) if x else line)
    out_ref[0, :, :128] = total.astype(BF16)
    out_ref[0, :, 128:] = jnp.zeros((ROWS, out_ref.shape[2] - 128), BF16)


def chosen(code, pieces):
    owned = pieces[0].shape[0]
    choice, local = code // owned, code % owned
    rows = jnp.zeros(pieces[0].shape[1:], BF16)
    for s, piece in enumerate(pieces):
        at = local if piece.shape[0] == owned else local % piece.shape[0]
        rows = jnp.where(choice == s, piece[at], rows)
    return rows


def code_of(ids_ref, x, z, core):
    return ids_ref[x, z, LANES * core + 3] * 32 + ids_ref[x, z, LANES * core + 4]


def pick_other_kernel(where_ref, ids_ref, f0, f1, f2a, f3, f2b, out_ref):
    core = 1 - where_ref[1]

    def step(z, carry):
        for x in range(X):
            code = code_of(ids_ref, x, z, core)
            out_ref[x * Z + z] = chosen(code, (f0, f1, f2a, f3, f2b))
        return carry

    lax.fori_loop(0, Z, step, 0, unroll=4)


def pick_own_kernel(where_ref, ids_ref, middle_ref, f0, f1, f2a, f3, f2b, out_ref):
    core = where_ref[1]
    middle_width = middle_ref.shape[2]

    def step(z, carry):
        for x in range(X):
            m = x * Z + z
            code = code_of(ids_ref, x, z, core)
            out_ref[m, :, :middle_width] = middle_ref[ids_ref[x, z, LANES * core]]
            out_ref[m, :, middle_width:] = chosen(code, (f0, f1, f2a, f3, f2b))
        return carry

    lax.fori_loop(0, Z, step, 0, unroll=4)


def merge_kernel(send_ref, extra_ref, out_ref):
    middle_width = send_ref.shape[2] - extra_ref.shape[2]
    out_ref[:, :, :middle_width] = send_ref[:, :, :middle_width]
    out_ref[:, :, middle_width:] = send_ref[:, :, middle_width:] + extra_ref[...]


def coarse_kernel(
    where_ref, ids_ref, x_ref, g_ref, ox_ref, og_ref, h0, h1, h2a, h2b, h3,
    s0, s1, s2a, s2b, s3, back_ref, other_back_ref, half_ref, own_term, other_term,
):
    y_index = where_ref[0]
    c_index, x_index, z_index = where_ref[1], where_ref[2], where_ref[3]
    own_id = ids_ref[x_index, z_index, LANES * c_index] // 16
    other_id = ids_ref[x_index, z_index, LANES * (1 - c_index)] // 16
    width = h0.shape[1] // 2

    def level(identity, inputs, upstream, term_ref, into_ref):
        choice = (y_index - identity + Y) % Y
        for s, ref in ((0, h0), (1, h1), (3, h3)):

            @pl.when(choice == s)
            def _(ref=ref):
                half_ref[...] = ref[...]

        @pl.when(choice == 2)
        def _():
            half_ref[: h2a.shape[0]] = h2a[...]
            half_ref[h2a.shape[0] :] = h2b[...]

        tokens, cotangent = inputs[...], upstream[...]
        before = dot(tokens, half_ref[:, :width], 1, 0)
        hidden_grad = dot(cotangent, half_ref[:, width:], 1, 0)
        hidden, before_grad = gelu_pair(before, hidden_grad)
        term_ref[:, :width] = dot(tokens, before_grad, 0, 0)
        term_ref[:, width:] = dot(cotangent, hidden, 0, 0)
        into_ref[...] = dot(before_grad, half_ref[:, :width], 1, 1)

    level(own_id, x_ref, g_ref, own_term, back_ref)
    level(other_id, ox_ref, og_ref, other_term, other_back_ref)
    middle_row = s2a.shape[0]
    everything = slice(0, s0.shape[0])
    lower, upper = slice(0, middle_row), slice(middle_row, s0.shape[0])
    for s, rows, ref in (
        (2, lower, s2a),
        (2, upper, s2b),
        (0, everything, s0),
        (1, everything, s1),
        (3, everything, s3),
    ):
        block = (y_index + s) % Y
        own, other = own_id == block, other_id == block

        @pl.when(jnp.logical_and(own, other))
        def _(ref=ref, rows=rows):
            ref[...] = (own_term[rows] + other_term[rows]).astype(BF16)

        @pl.when(jnp.logical_and(own, jnp.logical_not(other)))
        def _(ref=ref, rows=rows):
            ref[...] = own_term[rows].astype(BF16)

        @pl.when(jnp.logical_and(other, jnp.logical_not(own)))
        def _(ref=ref, rows=rows):
            ref[...] = other_term[rows].astype(BF16)

        @pl.when(jnp.logical_not(jnp.logical_or(own, other)))
        def _(ref=ref):
            ref[...] = jnp.zeros(ref.shape, BF16)


def coarse_relay_kernel(s1, s3, r1, r3, up_ref, down_ref):
    middle_row = r1.shape[0]
    up_ref[:middle_row] = (s1[:middle_row].astype(F32) + r1[...].astype(F32)).astype(BF16)
    up_ref[middle_row:] = s1[middle_row:]
    down_ref[:middle_row] = s3[:middle_row]
    down_ref[middle_row:] = (s3[middle_row:].astype(F32) + r3[...].astype(F32)).astype(BF16)


def coarse_sum_kernel(where_ref, s0, up_ref, down_ref, own_ref, *leaving):
    x_index = where_ref[2]
    rows = own_ref.shape[0]
    for s, ref in enumerate((own_ref,) + leaving):
        at = pl.ds(pl.multiple_of(((x_index + s) % X) * rows, rows), rows)
        total = s0[at].astype(F32) + up_ref[at].astype(F32) + down_ref[at].astype(F32)
        ref[...] = total.astype(ref.dtype)


def levels_kernel(x_ref, g_ref, w_ref, term_ref, back_ref):
    tokens, cotangent = x_ref[...], g_ref[...]
    middle = 256
    half = middle // 2
    before = dot(tokens, w_ref[:, :half], 1, 0)
    hidden_grad = dot(cotangent, w_ref[:, half:middle], 1, 0)
    hidden, before_grad = gelu_pair(before, hidden_grad)
    fine = w_ref[:, middle:]
    width = fine.shape[1]
    fine_before = dot(tokens, fine, 1, 0)
    fine_hidden_grad = pltpu.roll(dot(cotangent, fine, 1, 0), width // 2, 1)
    first = lax.broadcasted_iota(I32, fine_before.shape, 1) < width // 2
    fine_before = jnp.where(first, fine_before, 0.0)
    fine_hidden_grad = jnp.where(first, fine_hidden_grad, 0.0)
    fine_hidden, fine_before_grad = gelu_pair(fine_before, fine_hidden_grad)
    fine_hidden = pltpu.roll(fine_hidden.astype(F32), width // 2, 1).astype(BF16)
    term_ref[:, :half] = dot(tokens, before_grad, 0, 0).astype(BF16)
    term_ref[:, half:middle] = dot(cotangent, hidden, 0, 0).astype(BF16)
    term_ref[:, middle:] = (
        dot(tokens, fine_before_grad, 0, 0) + dot(cotangent, fine_hidden, 0, 0)
    ).astype(BF16)
    back_ref[...] = dot(before_grad, w_ref[:, :half], 1, 1) + dot(fine_before_grad, fine, 1, 1)


def collect_kernel(
    where_ref, ids_ref, numbers_ref, parts_ref, packet_ref, s0, s1, s3, sums_ref
):
    y_index, c_index = where_ref[0], where_ref[1]
    middle = parts_ref.shape[2] - 128
    slot = s0.shape[0]
    pairs = MEMBERS // 2
    sums_ref[...] = jnp.zeros(sums_ref.shape, F32)

    def step(zz, carry):
        for x in range(X):
            for h in range(2):
                z = 2 * zz + h
                block = ids_ref[x, z, LANES * c_index]
                place = ((block // slot - y_index + Y) % Y) * slot + block % slot
                m = x * Z + z
                sums_ref[place] = sums_ref[place] + parts_ref[m, :, :middle].astype(F32)
                pair = x * (Z // 2) + zz
                packet_ref[pair, :, h * 128 : h * 128 + 128] = parts_ref[m, :, middle:]
        return carry

    lax.fori_loop(0, Z // 2, step, 0)
    packet_ref[pairs] = numbers_ref[0]
    packet_ref[pairs + 1 :] = sums_ref[2 * slot : 3 * slot].astype(BF16)
    s0[...] = sums_ref[:slot]
    s1[...] = sums_ref[slot : 2 * slot]
    s3[...] = sums_ref[3 * slot :]


def relay_kernel(r1, r3, s1, s3, up_ref, down_ref):
    pairs = MEMBERS // 2
    lower = pairs // 2
    split = s1.shape[0] // 2
    middle = pairs + 1
    up_ref[:lower] = r1[:lower]
    up_ref[lower] = r1[pairs]
    up_ref[lower + 1 : lower + 1 + split] = (
        s1[:split] + r1[middle : middle + split].astype(F32)
    ).astype(BF16)
    up_ref[lower + 1 + split :] = s1[split:].astype(BF16)
    down_ref[:lower] = r3[lower:pairs]
    down_ref[lower : lower + split] = s3[:split].astype(BF16)
    down_ref[lower + split :] = (s3[split:] + r3[middle + split :].astype(F32)).astype(BF16)


def add_fine(where_ref, owned, ids_ref, p, piece, xs, sums_ref):
    y_index, c_index = where_ref[0], where_ref[1]

    def step(zz, carry):
        for x in xs:
            for h in range(2):
                place = LANES * (C * x + c_index)
                z = 2 * zz + h
                fine_id = ids_ref[p, z, place + 1] * 32 + ids_ref[p, z, place + 2]
                owner = fine_id // owned
                slot = ((owner + c_index) % C) * owned + fine_id % owned
                slot = jnp.where(owner // C == y_index, slot, C * owned)
                pair = (x - xs[0]) * (Z // 2) + zz
                part = piece[pair, :, h * 128 : h * 128 + 128]
                sums_ref[slot] = sums_ref[slot] + part.astype(F32)
        return carry

    lax.fori_loop(0, Z // 2, step, 0)


def first_fine_kernel(where_ref, ids_ref, p0, p1, p3, sums_ref):
    owned = (sums_ref.shape[0] - 8) // C
    sums_ref[...] = jnp.zeros(sums_ref.shape, F32)
    for p, piece in enumerate((p0, p1, p3)):
        add_fine(where_ref, owned, ids_ref, p, piece, range(X), sums_ref)


def middle_kernel(where_ref, s0, q1, q3, kept_ref, leave_ref):
    share = kept_ref.shape[0]
    lower = MEMBERS // 4

    def middle_of(side):
        low = side * share
        return (
            s0[pl.ds(low, share)]
            + q1[pl.ds(lower + 1 + low, share)].astype(F32)
            + q3[pl.ds(lower + low, share)].astype(F32)
        )

    kept_ref[...] = middle_of(where_ref[1])
    leave_ref[...] = middle_of(1 - where_ref[1]).astype(BF16)


def last_fine_kernel(
    where_ref, ids_ref, before_ref, q1, q3, leave_ref, fine_ref, sums_ref
):
    owned = fine_ref.shape[0]
    sums_ref[...] = before_ref[...]
    add_fine(where_ref, owned, ids_ref, 0, q1, range(X // 2), sums_ref)
    add_fine(where_ref, owned, ids_ref, 0, q3, range(X // 2, X), sums_ref)
    fine_ref[...] = sums_ref[:owned]
    half = owned // 2
    leave_ref[:, :, :128] = sums_ref[owned : owned + half].astype(BF16)
    leave_ref[:, :, 128:] = sums_ref[owned + half : 2 * owned].astype(BF16)


def done_kernel(kept_ref, arrived_ref, coarse_ref, out_ref):
    share = kept_ref.shape[0]
    middle = (kept_ref[...] + arrived_ref[...].astype(F32)).astype(BF16)
    coarse = coarse_ref[0].astype(F32)
    for z in range(1, Z):
        coarse = coarse + coarse_ref[z].astype(F32)
    coarse = coarse.astype(BF16)
    for g in range(out_ref.shape[0]):
        out_ref[g, :share] = middle
        out_ref[g, share] = coarse


def finish_kernel(fine_ref, arrived_ref, out_ref):
    half = fine_ref.shape[0] // 2
    for h in range(2):
        low = h * half
        out_ref[low : low + half] = (
            fine_ref[low : low + half]
            + arrived_ref[:, :, h * 128 : h * 128 + 128].astype(F32)
        ).astype(BF16)


def spread_kernel(total_ref, coarse_ref, middle_ref):
    share = total_ref.shape[1] - 1
    width = total_ref.shape[3] // 2
    for y in range(Y):
        for core in range(C):
            g = y * C + core
            middle_ref[g * share : (g + 1) * share] = total_ref[g, :share]
            low = core * width
            coarse_ref[y, :, low : low + width] = total_ref[g, share, :, :width]
            low = (C + core) * width
            coarse_ref[y, :, low : low + width] = total_ref[g, share, :, width:]


def on_device(tokens, cotangent, path, coarse_weights, middle_weights, fine_weights):
    y_index, c_index = lax.axis_index("y"), lax.axis_index("c")
    x_index = lax.axis_index("x")
    where = jnp.stack([y_index, c_index, x_index, lax.axis_index("z")]).astype(I32)
    fine_owned, _, fine_width = fine_weights.shape
    coarse_width = coarse_weights.shape[2]
    middle_width = middle_weights.shape[2]
    half = coarse_width // 2
    depth = MEMBERS * ROWS

    other_path = shift(path, "c", 1)
    packet = kernel_call(
        partial(packet_kernel, fine_owned),
        [SMEM, SMEM, SMEM, VMEM],
        bf16(Z, ROWS, half + 128),
    )(where, path, other_path, coarse_weights)
    packets = exchange(packet, "z")

    fine_one = shift(after(fine_weights, packet), "y", 1)
    fine_three = shift(after(fine_weights, packet), "y", 3)
    packets, fine_one = lax.optimization_barrier((packets, fine_one))
    packets = kernel_call(repack_kernel, [VMEM], bf16(X, Z * ROWS + ROWS, half))(packets)
    packets = exchange(packets, "x")
    split = fine_owned // 2
    fine_rows = [
        fine_weights,
        fine_one,
        shift(fine_one[:split], "y", 1),
        fine_three,
        shift(fine_three[split:], "y", 3),
    ]
    ids = packets[:, Z * ROWS : Z * ROWS + Z, : LANES * C].astype(I32)
    extra = kernel_call(
        pick_other_kernel, [SMEM] * 2 + [VMEM] * 5, bf16(MEMBERS, ROWS, fine_width)
    )(where, ids, *fine_rows)
    arrived = shift(extra, "c", 1)
    send = kernel_call(
        pick_own_kernel,
        [SMEM] * 2 + [VMEM] * 6,
        bf16(MEMBERS, ROWS, middle_width + fine_width),
    )(where, ids, middle_weights, *fine_rows)
    send = kernel_call(merge_kernel, [VMEM] * 2, bf16(*send.shape))(send, arrived)
    mine = exchange(send, ("x", "z")).reshape(depth, -1)

    both = jnp.concatenate([after(tokens, send), cotangent], axis=0)
    other_both = shift(both, "c", 1)

    lines = after(packets, send)[:, Z * ROWS :]
    numbers = kernel_call(numbers_kernel, [VMEM] * X, bf16(1, ROWS, 2 * fine_width))(
        *[lines[x] for x in range(X)]
    )
    block = after(packets, send)[:, : Z * ROWS].reshape(depth, half)
    one, three = shift(block, "y", 1), shift(block, "y", 3)
    middle_row = depth // 2
    halves = [
        block,
        one,
        shift(one[:middle_row], "y", 1),
        shift(three[middle_row:], "y", 3),
        three,
    ]
    length = tokens.shape[0]
    slots = kernel_call(
        coarse_kernel,
        [SMEM, SMEM] + [VMEM] * 9,
        tuple(
            [bf16(depth, half)] * 2
            + [bf16(middle_row, half)] * 2
            + [bf16(depth, half)]
            + [f32(length, depth)] * 2
        ),
        [
            pltpu.VMEM((depth, half), BF16),
            pltpu.VMEM((depth, half), F32),
            pltpu.VMEM((depth, half), F32),
        ],
        cost=10_000_000,
    )(
        where, ids, tokens, cotangent, other_both[:length], other_both[length:], *halves
    )
    near, ahead, far_low, far_high, behind, coarse_back, other_back = slots
    up, down = shift(far_low, "y", 1), shift(far_high, "y", 3)
    mine, numbers, up, down = lax.optimization_barrier((mine, numbers, up, down))

    terms, back = kernel_call(
        levels_kernel,
        [VMEM] * 3,
        (bf16(depth, middle_width + fine_width), f32(length, depth)),
        cost=10_000_000,
    )(tokens, cotangent, mine)
    parts = exchange(terms.reshape(MEMBERS, ROWS, -1), ("x", "z"))

    up, down = kernel_call(coarse_relay_kernel, [VMEM] * 4, (bf16(depth, half),) * 2)(
        ahead, behind, up, down
    )
    up, down = shift(after(up, terms), "y", 1), shift(after(down, terms), "y", 3)
    column_sum, *leaving = kernel_call(
        coarse_sum_kernel,
        [SMEM] + [VMEM] * 3,
        tuple([f32(Z * ROWS, half)] + [bf16(Z * ROWS, half)] * (X - 1)),
    )(where, near, up, down)
    for s in range(1, X):
        column_sum = column_sum + shift(leaving[s - 1], "x", s).astype(F32)
    column_sum = column_sum.astype(BF16).reshape(Z, ROWS, half)
    parts, column_sum = lax.optimization_barrier((parts, column_sum))

    middle_count = middle_weights.shape[0]
    pairs = MEMBERS // 2
    lower = pairs // 2
    quarter_count = middle_count // Y
    share = quarter_count // C
    first, s0, s1, s3 = kernel_call(
        collect_kernel,
        [SMEM, SMEM, VMEM, VMEM],
        tuple(
            [bf16(pairs + 1 + quarter_count, ROWS, middle_width)]
            + [f32(quarter_count, ROWS, middle_width)] * 3
        ),
        [pltpu.VMEM((middle_count, ROWS, middle_width), F32)],
    )(where, ids, numbers, parts)
    r1, r3 = shift(first, "y", 1), shift(first, "y", 3)
    coarse_four = exchange(after(column_sum, first), "z")
    second = kernel_call(
        relay_kernel,
        [VMEM] * 4,
        (
            bf16(lower + 1 + quarter_count, ROWS, middle_width),
            bf16(lower + quarter_count, ROWS, middle_width),
        ),
    )(r1, r3, s1, s3)
    q1, q3 = shift(second[0], "y", 1), shift(second[1], "y", 3)
    fine_ids = [f[pairs, :Z, : LANES * C * X].astype(I32) for f in (first, r1, r3)]
    fine_sums = kernel_call(
        first_fine_kernel,
        [SMEM, SMEM] + [VMEM] * 3,
        f32(C * fine_owned + 8, ROWS, fine_width),
    )(where, jnp.stack(fine_ids), first, r1, r3)
    fine_sums, q1, q3, coarse_four = lax.optimization_barrier(
        (fine_sums, q1, q3, coarse_four)
    )
    middle_kept, middle_leave = kernel_call(
        middle_kernel,
        [SMEM] + [VMEM] * 3,
        (f32(share, ROWS, middle_width), bf16(share, ROWS, middle_width)),
    )(where, s0, q1, q3)
    middle_arrived = shift(middle_leave, "c", 1)
    fine_leave, fine_kept = kernel_call(
        last_fine_kernel,
        [SMEM, SMEM] + [VMEM] * 3,
        (bf16(fine_owned // 2, ROWS, 2 * fine_width), f32(fine_owned, ROWS, fine_width)),
        [pltpu.VMEM((C * fine_owned + 8, ROWS, fine_width), F32)],
    )(where, q1[lower, :Z, : LANES * C * X].astype(I32)[None], fine_sums, q1, q3)
    done = kernel_call(
        done_kernel, [VMEM] * 3, bf16(Y * C, share + 1, ROWS, middle_width)
    )(middle_kept, middle_arrived, coarse_four)
    total = exchange(done, ("y", "c"))
    fine_arrived = shift(after(fine_leave, done), "c", 1)
    coarse_total, middle_total = kernel_call(
        spread_kernel, [VMEM], (bf16(*coarse_weights.shape), bf16(*middle_weights.shape))
    )(total)
    fine_total = kernel_call(
        finish_kernel, [VMEM] * 2, bf16(fine_owned, ROWS, fine_width)
    )(fine_kept, fine_arrived)
    other_back = shift(after(other_back, second[0]), "c", 1)
    tokens_grad = (coarse_back + other_back + back).astype(BF16)
    return (tokens_grad, coarse_total, middle_total, fine_total)


def solution(mesh):
    fine_mesh = Mesh(mesh.devices.reshape(Y, C, X, Z), EVERYONE)
    members = ("x", "z")
    return jax.shard_map(
        on_device,
        mesh=fine_mesh,
        in_specs=(
            P(EVERYONE, None),
            P(EVERYONE, None),
            P(EVERYONE, None),
            P(None, members, None),
            P(None, members, None),
            P(("y", "c"), members, None),
        ),
        out_specs=(
            P(EVERYONE, None),
            P(None, members, None),
            P(None, members, None),
            P(("y", "c"), members, None),
        ),
        check_vma=False,
    )
```

```python
from functools import partial

import jax
import jax.numpy as jnp
from jax import lax
from jax.experimental import pallas as pl
from jax.experimental.pallas import tpu as pltpu
from jax.sharding import Mesh, PartitionSpec as P

F32 = jnp.float32
BF16 = jnp.bfloat16
I32 = jnp.int32
Y, C, X, Z = 4, 2, 4, 16
MEMBERS = X * Z
ROWS = 16
LANES = 8
EVERYONE = ("y", "c", "x", "z")
VMEM = pl.BlockSpec(memory_space=pltpu.VMEM)
SMEM = pl.BlockSpec(memory_space=pltpu.SMEM)


def exchange(array, axes):
    return lax.all_to_all(array, axes, split_axis=0, concat_axis=0, tiled=True)


def gather(array, axes):
    count = lax.axis_size(axes)
    return exchange(jnp.broadcast_to(array[None], (count,) + array.shape), axes)


def shift(array, axis, step):
    count = lax.axis_size(axis)
    return lax.ppermute(array, axis, [(i, (i + step) % count) for i in range(count)])


def after(array, *others):
    return lax.optimization_barrier((array,) + others)[0]


def kernel_call(body, in_specs, out_shape, scratch=(), cost=1_000_000, limit=16):
    return pl.pallas_call(
        body,
        out_shape=out_shape,
        in_specs=in_specs,
        out_specs=jax.tree.map(lambda _: VMEM, out_shape),
        scratch_shapes=list(scratch),
        compiler_params=pltpu.CompilerParams(vmem_limit_bytes=limit * 1024 * 1024),
        cost_estimate=pl.CostEstimate(flops=cost, bytes_accessed=cost, transcendentals=0),
    )


def bf16(*shape):
    return jax.ShapeDtypeStruct(shape, BF16)


def f32(*shape):
    return jax.ShapeDtypeStruct(shape, F32)


def dot(left, right, left_dim, right_dim):
    return lax.dot_general(
        left, right, (((left_dim,), (right_dim,)), ((), ())), preferred_element_type=F32
    )


def gelu_pair(v, upstream):
    scale = 0.7978845608028654
    square = v * v
    t = jnp.tanh(scale * (v + 0.044715 * (square * v)))
    half = 0.5 * (1.0 + t)
    slope = half + 0.5 * v * (1.0 - t * t) * (scale * (1.0 + 0.134145 * square))
    return (v * half).astype(BF16), (upstream * slope).astype(BF16)


def packet_kernel(owned, where_ref, own_ref, other_ref, coarse_ref, out_ref):
    y_index, c_index = where_ref[0], where_ref[1]
    width = coarse_ref.shape[2] // 4
    up = coarse_ref[y_index, :, pl.ds(pl.multiple_of(c_index * width, width), width)]
    down = coarse_ref[
        y_index, :, pl.ds(pl.multiple_of((c_index + 2) * width, width), width)
    ]
    lanes = lax.broadcasted_iota(I32, (ROWS, 128), 1)
    numbers = jnp.zeros((ROWS, 128), F32)
    for core, ref in ((c_index, own_ref), (1 - c_index, other_ref)):
        fine_id = ref[0, 2]
        owner, slot = fine_id // owned, fine_id % owned
        choice = (y_index - owner // C + Y) % Y
        choice = jnp.where(jnp.logical_and(choice == 2, slot >= owned // 2), Y, choice)
        choice = jnp.where(owner % C == c_index, choice, Y + 1)
        code = choice * owned + slot
        values = (ref[0, 1], fine_id // 32, fine_id % 32, code // 32, code % 32)
        for i, value in enumerate(values):
            numbers = jnp.where(lanes == LANES * core + i, value.astype(F32), numbers)
    numbers = numbers.astype(BF16)
    for z in range(Z):
        out_ref[z, :, :width] = up
        out_ref[z, :, width : 2 * width] = down
        out_ref[z, :, 2 * width :] = numbers


def repack_kernel(packets_ref, out_ref):
    width = out_ref.shape[2]
    rows = lax.broadcasted_iota(I32, (ROWS, 128), 0)
    line = jnp.zeros((ROWS, 128), F32)
    for z in range(Z):
        line = jnp.where(rows == z, packets_ref[z, :, width:].astype(F32), line)
    line = line.astype(BF16)
    for x in range(X):
        for z in range(Z):
            out_ref[x, z * ROWS : (z + 1) * ROWS] = packets_ref[z, :, :width]
        out_ref[x, Z * ROWS :, :128] = line
        out_ref[x, Z * ROWS :, 128:] = jnp.zeros((ROWS, width - 128), BF16)


def numbers_kernel(*refs):
    lines, out_ref = refs[:-1], refs[-1]
    total = jnp.zeros((ROWS, 128), F32)
    for x, ref in enumerate(lines):
        line = ref[:, :128].astype(F32)
        total = total + (pltpu.roll(line, LANES * C * x, 1) if x else line)
    out_ref[0, :, :128] = total.astype(BF16)
    out_ref[0, :, 128:] = jnp.zeros((ROWS, out_ref.shape[2] - 128), BF16)


def chosen(code, pieces):
    owned = pieces[0].shape[0]
    choice, local = code // owned, code % owned
    rows = jnp.zeros(pieces[0].shape[1:], BF16)
    for s, piece in enumerate(pieces):
        at = local if piece.shape[0] == owned else local % piece.shape[0]
        rows = jnp.where(choice == s, piece[at], rows)
    return rows


def code_of(ids_ref, x, z, core):
    return ids_ref[x, z, LANES * core + 3] * 32 + ids_ref[x, z, LANES * core + 4]


def pick_other_kernel(where_ref, ids_ref, f0, f1, f2a, f3, f2b, out_ref):
    core = 1 - where_ref[1]

    def step(z, carry):
        for x in range(X):
            code = code_of(ids_ref, x, z, core)
            out_ref[x * Z + z] = chosen(code, (f0, f1, f2a, f3, f2b))
        return carry

    lax.fori_loop(0, Z, step, 0, unroll=4)


def pick_own_kernel(where_ref, ids_ref, middle_ref, f0, f1, f2a, f3, f2b, out_ref):
    core = where_ref[1]
    middle_width = middle_ref.shape[2]

    def step(z, carry):
        for x in range(X):
            m = x * Z + z
            code = code_of(ids_ref, x, z, core)
            out_ref[m, :, :middle_width] = middle_ref[ids_ref[x, z, LANES * core]]
            out_ref[m, :, middle_width:] = chosen(code, (f0, f1, f2a, f3, f2b))
        return carry

    lax.fori_loop(0, Z, step, 0, unroll=4)


def merge_kernel(send_ref, extra_ref, out_ref):
    middle_width = send_ref.shape[2] - extra_ref.shape[2]
    out_ref[:, :, :middle_width] = send_ref[:, :, :middle_width]
    out_ref[:, :, middle_width:] = send_ref[:, :, middle_width:] + extra_ref[...]


def coarse_kernel(
    where_ref, ids_ref, x_ref, g_ref, ox_ref, og_ref, h0, h1, h2a, h2b, h3,
    s0, s1, s2a, s2b, s3, back_ref, other_back_ref, half_ref, own_term, other_term,
):
    y_index = where_ref[0]
    c_index, x_index, z_index = where_ref[1], where_ref[2], where_ref[3]
    own_id = ids_ref[x_index, z_index, LANES * c_index] // 16
    other_id = ids_ref[x_index, z_index, LANES * (1 - c_index)] // 16
    width = h0.shape[1] // 2

    def level(identity, inputs, upstream, term_ref, into_ref):
        choice = (y_index - identity + Y) % Y
        for s, ref in ((0, h0), (1, h1), (3, h3)):

            @pl.when(choice == s)
            def _(ref=ref):
                half_ref[...] = ref[...]

        @pl.when(choice == 2)
        def _():
            half_ref[: h2a.shape[0]] = h2a[...]
            half_ref[h2a.shape[0] :] = h2b[...]

        tokens, cotangent = inputs[...], upstream[...]
        before = dot(tokens, half_ref[:, :width], 1, 0)
        hidden_grad = dot(cotangent, half_ref[:, width:], 1, 0)
        hidden, before_grad = gelu_pair(before, hidden_grad)
        term_ref[:, :width] = dot(tokens, before_grad, 0, 0)
        term_ref[:, width:] = dot(cotangent, hidden, 0, 0)
        into_ref[...] = dot(before_grad, half_ref[:, :width], 1, 1)

    level(own_id, x_ref, g_ref, own_term, back_ref)
    level(other_id, ox_ref, og_ref, other_term, other_back_ref)
    middle_row = s2a.shape[0]
    everything = slice(0, s0.shape[0])
    lower, upper = slice(0, middle_row), slice(middle_row, s0.shape[0])
    for s, rows, ref in (
        (2, lower, s2a),
        (2, upper, s2b),
        (0, everything, s0),
        (1, everything, s1),
        (3, everything, s3),
    ):
        block = (y_index + s) % Y
        own, other = own_id == block, other_id == block

        @pl.when(jnp.logical_and(own, other))
        def _(ref=ref, rows=rows):
            ref[...] = (own_term[rows] + other_term[rows]).astype(BF16)

        @pl.when(jnp.logical_and(own, jnp.logical_not(other)))
        def _(ref=ref, rows=rows):
            ref[...] = own_term[rows].astype(BF16)

        @pl.when(jnp.logical_and(other, jnp.logical_not(own)))
        def _(ref=ref, rows=rows):
            ref[...] = other_term[rows].astype(BF16)

        @pl.when(jnp.logical_not(jnp.logical_or(own, other)))
        def _(ref=ref):
            ref[...] = jnp.zeros(ref.shape, BF16)


def coarse_relay_kernel(s1, s3, r1, r3, up_ref, down_ref):
    middle_row = r1.shape[0]
    up_ref[:middle_row] = (s1[:middle_row].astype(F32) + r1[...].astype(F32)).astype(BF16)
    up_ref[middle_row:] = s1[middle_row:]
    down_ref[:middle_row] = s3[:middle_row]
    down_ref[middle_row:] = (s3[middle_row:].astype(F32) + r3[...].astype(F32)).astype(BF16)


def coarse_sum_kernel(where_ref, s0, up_ref, down_ref, own_ref, *leaving):
    x_index = where_ref[2]
    rows = own_ref.shape[0]
    for s, ref in enumerate((own_ref,) + leaving):
        at = pl.ds(pl.multiple_of(((x_index + s) % X) * rows, rows), rows)
        total = s0[at].astype(F32) + up_ref[at].astype(F32) + down_ref[at].astype(F32)
        ref[...] = total.astype(ref.dtype)


def levels_kernel(x_ref, g_ref, w_ref, term_ref, back_ref):
    tokens, cotangent = x_ref[...], g_ref[...]
    middle = 256
    half = middle // 2
    before = dot(tokens, w_ref[:, :half], 1, 0)
    hidden_grad = dot(cotangent, w_ref[:, half:middle], 1, 0)
    hidden, before_grad = gelu_pair(before, hidden_grad)
    fine = w_ref[:, middle:]
    width = fine.shape[1]
    fine_before = dot(tokens, fine, 1, 0)
    fine_hidden_grad = pltpu.roll(dot(cotangent, fine, 1, 0), width // 2, 1)
    first = lax.broadcasted_iota(I32, fine_before.shape, 1) < width // 2
    fine_before = jnp.where(first, fine_before, 0.0)
    fine_hidden_grad = jnp.where(first, fine_hidden_grad, 0.0)
    fine_hidden, fine_before_grad = gelu_pair(fine_before, fine_hidden_grad)
    fine_hidden = pltpu.roll(fine_hidden.astype(F32), width // 2, 1).astype(BF16)
    term_ref[:, :half] = dot(tokens, before_grad, 0, 0).astype(BF16)
    term_ref[:, half:middle] = dot(cotangent, hidden, 0, 0).astype(BF16)
    term_ref[:, middle:] = (
        dot(tokens, fine_before_grad, 0, 0) + dot(cotangent, fine_hidden, 0, 0)
    ).astype(BF16)
    back_ref[...] = dot(before_grad, w_ref[:, :half], 1, 1) + dot(fine_before_grad, fine, 1, 1)


def collect_kernel(
    where_ref, ids_ref, numbers_ref, parts_ref, packet_ref, s0, s1, s3, sums_ref
):
    y_index, c_index = where_ref[0], where_ref[1]
    middle = parts_ref.shape[2] - 128
    slot = s0.shape[0]
    pairs = MEMBERS // 2
    sums_ref[...] = jnp.zeros(sums_ref.shape, F32)

    def step(zz, carry):
        for x in range(X):
            for h in range(2):
                z = 2 * zz + h
                block = ids_ref[x, z, LANES * c_index]
                place = ((block // slot - y_index + Y) % Y) * slot + block % slot
                m = x * Z + z
                sums_ref[place] = sums_ref[place] + parts_ref[m, :, :middle].astype(F32)
                pair = x * (Z // 2) + zz
                packet_ref[pair, :, h * 128 : h * 128 + 128] = parts_ref[m, :, middle:]
        return carry

    lax.fori_loop(0, Z // 2, step, 0)
    packet_ref[pairs] = numbers_ref[0]
    packet_ref[pairs + 1 :] = sums_ref[2 * slot : 3 * slot].astype(BF16)
    s0[...] = sums_ref[:slot]
    s1[...] = sums_ref[slot : 2 * slot]
    s3[...] = sums_ref[3 * slot :]


def relay_kernel(r1, r3, s1, s3, up_ref, down_ref):
    pairs = MEMBERS // 2
    lower = pairs // 2
    split = s1.shape[0] // 2
    middle = pairs + 1
    up_ref[:lower] = r1[:lower]
    up_ref[lower] = r1[pairs]
    up_ref[lower + 1 : lower + 1 + split] = (
        s1[:split] + r1[middle : middle + split].astype(F32)
    ).astype(BF16)
    up_ref[lower + 1 + split :] = s1[split:].astype(BF16)
    down_ref[:lower] = r3[lower:pairs]
    down_ref[lower : lower + split] = s3[:split].astype(BF16)
    down_ref[lower + split :] = (s3[split:] + r3[middle + split :].astype(F32)).astype(BF16)


def add_fine(where_ref, owned, ids_ref, p, piece, xs, sums_ref):
    y_index, c_index = where_ref[0], where_ref[1]

    def step(zz, carry):
        for x in xs:
            for h in range(2):
                place = LANES * (C * x + c_index)
                z = 2 * zz + h
                fine_id = ids_ref[p, z, place + 1] * 32 + ids_ref[p, z, place + 2]
                owner = fine_id // owned
                slot = ((owner + c_index) % C) * owned + fine_id % owned
                slot = jnp.where(owner // C == y_index, slot, C * owned)
                pair = (x - xs[0]) * (Z // 2) + zz
                part = piece[pair, :, h * 128 : h * 128 + 128]
                sums_ref[slot] = sums_ref[slot] + part.astype(F32)
        return carry

    lax.fori_loop(0, Z // 2, step, 0)


def first_fine_kernel(where_ref, ids_ref, p0, p1, p3, sums_ref):
    owned = (sums_ref.shape[0] - 8) // C
    sums_ref[...] = jnp.zeros(sums_ref.shape, F32)
    for p, piece in enumerate((p0, p1, p3)):
        add_fine(where_ref, owned, ids_ref, p, piece, range(X), sums_ref)


def middle_kernel(where_ref, s0, q1, q3, kept_ref, leave_ref):
    share = kept_ref.shape[0]
    lower = MEMBERS // 4

    def middle_of(side):
        low = side * share
        return (
            s0[pl.ds(low, share)]
            + q1[pl.ds(lower + 1 + low, share)].astype(F32)
            + q3[pl.ds(lower + low, share)].astype(F32)
        )

    kept_ref[...] = middle_of(where_ref[1])
    leave_ref[...] = middle_of(1 - where_ref[1]).astype(BF16)


def last_fine_kernel(
    where_ref, ids_ref, before_ref, q1, q3, leave_ref, fine_ref, sums_ref
):
    owned = fine_ref.shape[0]
    sums_ref[...] = before_ref[...]
    add_fine(where_ref, owned, ids_ref, 0, q1, range(X // 2), sums_ref)
    add_fine(where_ref, owned, ids_ref, 0, q3, range(X // 2, X), sums_ref)
    fine_ref[...] = sums_ref[:owned]
    half = owned // 2
    leave_ref[:, :, :128] = sums_ref[owned : owned + half].astype(BF16)
    leave_ref[:, :, 128:] = sums_ref[owned + half : 2 * owned].astype(BF16)


def coarse_done_kernel(coarse_ref, out_ref):
    coarse = coarse_ref[0].astype(F32)
    for z in range(1, Z):
        coarse = coarse + coarse_ref[z].astype(F32)
    out_ref[...] = coarse.astype(BF16)


def done_kernel(kept_ref, arrived_ref, coarse_ref, out_ref):
    share = kept_ref.shape[0]
    middle = (kept_ref[...] + arrived_ref[...].astype(F32)).astype(BF16)
    coarse = coarse_ref[...]
    for g in range(out_ref.shape[0]):
        out_ref[g, :share] = middle
        out_ref[g, share] = coarse


def finish_kernel(fine_ref, arrived_ref, out_ref):
    half = fine_ref.shape[0] // 2
    for h in range(2):
        low = h * half
        out_ref[low : low + half] = (
            fine_ref[low : low + half]
            + arrived_ref[:, :, h * 128 : h * 128 + 128].astype(F32)
        ).astype(BF16)


def spread_kernel(total_ref, coarse_ref, middle_ref):
    share = total_ref.shape[1] - 1
    width = total_ref.shape[3] // 2
    for y in range(Y):
        for core in range(C):
            g = y * C + core
            middle_ref[g * share : (g + 1) * share] = total_ref[g, :share]
            low = core * width
            coarse_ref[y, :, low : low + width] = total_ref[g, share, :, :width]
            low = (C + core) * width
            coarse_ref[y, :, low : low + width] = total_ref[g, share, :, width:]


def on_device(tokens, cotangent, path, coarse_weights, middle_weights, fine_weights):
    y_index, c_index = lax.axis_index("y"), lax.axis_index("c")
    x_index = lax.axis_index("x")
    where = jnp.stack([y_index, c_index, x_index, lax.axis_index("z")]).astype(I32)
    fine_owned, _, fine_width = fine_weights.shape
    coarse_width = coarse_weights.shape[2]
    middle_width = middle_weights.shape[2]
    half = coarse_width // 2
    depth = MEMBERS * ROWS

    other_path = shift(path, "c", 1)
    packet = kernel_call(
        partial(packet_kernel, fine_owned),
        [SMEM, SMEM, SMEM, VMEM],
        bf16(Z, ROWS, half + 128),
    )(where, path, other_path, coarse_weights)
    packets = exchange(packet, "z")

    fine_one = shift(fine_weights, "y", 1)
    fine_three = shift(after(fine_weights, packet), "y", 3)
    split = fine_owned // 2
    fine_two = shift(fine_one[:split], "y", 1)
    packets, fine_one, fine_two, fine_three = lax.optimization_barrier((packets, fine_one, fine_two, fine_three))
    packets = kernel_call(repack_kernel, [VMEM], bf16(X, Z * ROWS + ROWS, half))(packets)
    packets = exchange(packets, "x")
    fine_rows = [
        fine_weights,
        fine_one,
        fine_two,
        fine_three,
        shift(fine_three[split:], "y", 3),
    ]
    ids = packets[:, Z * ROWS : Z * ROWS + Z, : LANES * C].astype(I32)
    extra = kernel_call(
        pick_other_kernel, [SMEM] * 2 + [VMEM] * 5, bf16(MEMBERS, ROWS, fine_width)
    )(where, ids, *fine_rows)
    arrived = shift(extra, "c", 1)
    send = kernel_call(
        pick_own_kernel,
        [SMEM] * 2 + [VMEM] * 6,
        bf16(MEMBERS, ROWS, middle_width + fine_width),
    )(where, ids, middle_weights, *fine_rows)
    send = kernel_call(merge_kernel, [VMEM] * 2, bf16(*send.shape))(send, arrived)
    mine = exchange(send, ("x", "z")).reshape(depth, -1)

    both = jnp.concatenate([after(tokens, send), cotangent], axis=0)
    other_both = shift(both, "c", 1)

    lines = after(packets, send)[:, Z * ROWS :]
    numbers = kernel_call(numbers_kernel, [VMEM] * X, bf16(1, ROWS, 2 * fine_width))(
        *[lines[x] for x in range(X)]
    )
    block = after(packets, send)[:, : Z * ROWS].reshape(depth, half)
    one, three = shift(block, "y", 1), shift(block, "y", 3)
    middle_row = depth // 2
    halves = [
        block,
        one,
        shift(one[:middle_row], "y", 1),
        shift(three[middle_row:], "y", 3),
        three,
    ]
    length = tokens.shape[0]
    slots = kernel_call(
        coarse_kernel,
        [SMEM, SMEM] + [VMEM] * 9,
        tuple(
            [bf16(depth, half)] * 2
            + [bf16(middle_row, half)] * 2
            + [bf16(depth, half)]
            + [f32(length, depth)] * 2
        ),
        [
            pltpu.VMEM((depth, half), BF16),
            pltpu.VMEM((depth, half), F32),
            pltpu.VMEM((depth, half), F32),
        ],
        cost=10_000_000,
    )(
        where, ids, tokens, cotangent, other_both[:length], other_both[length:], *halves
    )
    near, ahead, far_low, far_high, behind, coarse_back, other_back = slots
    up, down = shift(far_low, "y", 1), shift(far_high, "y", 3)
    mine, numbers, up, down = lax.optimization_barrier((mine, numbers, up, down))

    terms, back = kernel_call(
        levels_kernel,
        [VMEM] * 3,
        (bf16(depth, middle_width + fine_width), f32(length, depth)),
        cost=10_000_000,
    )(tokens, cotangent, mine)
    parts = exchange(terms.reshape(MEMBERS, ROWS, -1), ("x", "z"))

    up, down = kernel_call(coarse_relay_kernel, [VMEM] * 4, (bf16(depth, half),) * 2)(
        ahead, behind, up, down
    )
    up, down = shift(after(up, terms), "y", 1), shift(after(down, terms), "y", 3)
    column_sum, *leaving = kernel_call(
        coarse_sum_kernel,
        [SMEM] + [VMEM] * 3,
        tuple([f32(Z * ROWS, half)] + [bf16(Z * ROWS, half)] * (X - 1)),
    )(where, near, up, down)
    for s in range(1, X):
        column_sum = column_sum + shift(leaving[s - 1], "x", s).astype(F32)
    column_sum = column_sum.astype(BF16).reshape(Z, ROWS, half)
    other_back = shift(after(other_back, column_sum), "c", 1)
    parts, column_sum, other_back = lax.optimization_barrier((parts, column_sum, other_back))

    middle_count = middle_weights.shape[0]
    pairs = MEMBERS // 2
    lower = pairs // 2
    quarter_count = middle_count // Y
    share = quarter_count // C
    first, s0, s1, s3 = kernel_call(
        collect_kernel,
        [SMEM, SMEM, VMEM, VMEM],
        tuple(
            [bf16(pairs + 1 + quarter_count, ROWS, middle_width)]
            + [f32(quarter_count, ROWS, middle_width)] * 3
        ),
        [pltpu.VMEM((middle_count, ROWS, middle_width), F32)],
    )(where, ids, numbers, parts)
    r1, r3 = shift(first, "y", 1), shift(first, "y", 3)
    coarse_four = exchange(after(column_sum, first), "z")
    second = kernel_call(
        relay_kernel,
        [VMEM] * 4,
        (
            bf16(lower + 1 + quarter_count, ROWS, middle_width),
            bf16(lower + quarter_count, ROWS, middle_width),
        ),
    )(r1, r3, s1, s3)
    q1, q3 = shift(second[0], "y", 1), shift(second[1], "y", 3)
    fine_ids = [f[pairs, :Z, : LANES * C * X].astype(I32) for f in (first, r1, r3)]
    fine_sums = kernel_call(
        first_fine_kernel,
        [SMEM, SMEM] + [VMEM] * 3,
        f32(C * fine_owned + 8, ROWS, fine_width),
    )(where, jnp.stack(fine_ids), first, r1, r3)
    fine_sums, q1, q3, coarse_four = lax.optimization_barrier(
        (fine_sums, q1, q3, coarse_four)
    )
    middle_kept, middle_leave = kernel_call(
        middle_kernel,
        [SMEM] + [VMEM] * 3,
        (f32(share, ROWS, middle_width), bf16(share, ROWS, middle_width)),
    )(where, s0, q1, q3)
    middle_arrived = shift(middle_leave, "c", 1)
    fine_leave, fine_kept = kernel_call(
        last_fine_kernel,
        [SMEM, SMEM] + [VMEM] * 3,
        (bf16(fine_owned // 2, ROWS, 2 * fine_width), f32(fine_owned, ROWS, fine_width)),
        [pltpu.VMEM((C * fine_owned + 8, ROWS, fine_width), F32)],
    )(where, q1[lower, :Z, : LANES * C * X].astype(I32)[None], fine_sums, q1, q3)
    coarse_done = kernel_call(coarse_done_kernel, [VMEM], bf16(ROWS, half))(coarse_four)
    done = kernel_call(
        done_kernel, [VMEM] * 3, bf16(Y * C, share + 1, ROWS, middle_width)
    )(middle_kept, middle_arrived, coarse_done)
    total = exchange(done, ("y", "c"))
    fine_arrived = shift(after(fine_leave, done), "c", 1)
    coarse_total, middle_total = kernel_call(
        spread_kernel, [VMEM], (bf16(*coarse_weights.shape), bf16(*middle_weights.shape))
    )(total)
    fine_total = kernel_call(
        finish_kernel, [VMEM] * 2, bf16(fine_owned, ROWS, fine_width)
    )(fine_kept, fine_arrived)
    tokens_grad = (coarse_back + other_back + back).astype(BF16)
    return (tokens_grad, coarse_total, middle_total, fine_total)


def solution(mesh):
    fine_mesh = Mesh(mesh.devices.reshape(Y, C, X, Z), EVERYONE)
    members = ("x", "z")
    return jax.shard_map(
        on_device,
        mesh=fine_mesh,
        in_specs=(
            P(EVERYONE, None),
            P(EVERYONE, None),
            P(EVERYONE, None),
            P(None, members, None),
            P(None, members, None),
            P(("y", "c"), members, None),
        ),
        out_specs=(
            P(EVERYONE, None),
            P(None, members, None),
            P(None, members, None),
            P(("y", "c"), members, None),
        ),
        check_vma=False,
    )
```

```python
from functools import partial

import jax
import jax.numpy as jnp
from jax import lax
from jax.experimental import pallas as pl
from jax.experimental.pallas import tpu as pltpu
from jax.sharding import Mesh, PartitionSpec as P

F32 = jnp.float32
BF16 = jnp.bfloat16
I32 = jnp.int32
Y, C, X, Z = 4, 2, 4, 16
MEMBERS = X * Z
ROWS = 16
LANES = 8
EVERYONE = ("y", "c", "x", "z")
VMEM = pl.BlockSpec(memory_space=pltpu.VMEM)
SMEM = pl.BlockSpec(memory_space=pltpu.SMEM)


def exchange(array, axes):
    return lax.all_to_all(array, axes, split_axis=0, concat_axis=0, tiled=True)


def gather(array, axes):
    count = lax.axis_size(axes)
    return exchange(jnp.broadcast_to(array[None], (count,) + array.shape), axes)


def shift(array, axis, step):
    count = lax.axis_size(axis)
    return lax.ppermute(array, axis, [(i, (i + step) % count) for i in range(count)])


def after(array, *others):
    return lax.optimization_barrier((array,) + others)[0]


def kernel_call(body, in_specs, out_shape, scratch=(), cost=1_000_000, limit=16):
    return pl.pallas_call(
        body,
        out_shape=out_shape,
        in_specs=in_specs,
        out_specs=jax.tree.map(lambda _: VMEM, out_shape),
        scratch_shapes=list(scratch),
        compiler_params=pltpu.CompilerParams(vmem_limit_bytes=limit * 1024 * 1024),
        cost_estimate=pl.CostEstimate(flops=cost, bytes_accessed=cost, transcendentals=0),
    )


def bf16(*shape):
    return jax.ShapeDtypeStruct(shape, BF16)


def f32(*shape):
    return jax.ShapeDtypeStruct(shape, F32)


def dot(left, right, left_dim, right_dim):
    return lax.dot_general(
        left, right, (((left_dim,), (right_dim,)), ((), ())), preferred_element_type=F32
    )


def gelu_pair(v, upstream):
    scale = 0.7978845608028654
    square = v * v
    t = jnp.tanh(scale * (v + 0.044715 * (square * v)))
    half = 0.5 * (1.0 + t)
    slope = half + 0.5 * v * (1.0 - t * t) * (scale * (1.0 + 0.134145 * square))
    return (v * half).astype(BF16), (upstream * slope).astype(BF16)


def packet_kernel(owned, where_ref, own_ref, other_ref, coarse_ref, out_ref):
    y_index, c_index = where_ref[0], where_ref[1]
    width = coarse_ref.shape[2] // 4
    up = coarse_ref[y_index, :, pl.ds(pl.multiple_of(c_index * width, width), width)]
    down = coarse_ref[
        y_index, :, pl.ds(pl.multiple_of((c_index + 2) * width, width), width)
    ]
    lanes = lax.broadcasted_iota(I32, (ROWS, 128), 1)
    numbers = jnp.zeros((ROWS, 128), F32)
    for core, ref in ((c_index, own_ref), (1 - c_index, other_ref)):
        fine_id = ref[0, 2]
        owner, slot = fine_id // owned, fine_id % owned
        choice = (y_index - owner // C + Y) % Y
        choice = jnp.where(jnp.logical_and(choice == 2, slot >= owned // 2), Y, choice)
        choice = jnp.where(owner % C == c_index, choice, Y + 1)
        code = choice * owned + slot
        values = (ref[0, 1], fine_id // 32, fine_id % 32, code // 32, code % 32)
        for i, value in enumerate(values):
            numbers = jnp.where(lanes == LANES * core + i, value.astype(F32), numbers)
    numbers = numbers.astype(BF16)
    for z in range(Z):
        out_ref[z, :, :width] = up
        out_ref[z, :, width : 2 * width] = down
        out_ref[z, :, 2 * width :] = numbers


def repack_kernel(packets_ref, out_ref):
    width = out_ref.shape[2]
    rows = lax.broadcasted_iota(I32, (ROWS, 128), 0)
    line = jnp.zeros((ROWS, 128), F32)
    for z in range(Z):
        line = jnp.where(rows == z, packets_ref[z, :, width:].astype(F32), line)
    line = line.astype(BF16)
    for x in range(X):
        for z in range(Z):
            out_ref[x, z * ROWS : (z + 1) * ROWS] = packets_ref[z, :, :width]
        out_ref[x, Z * ROWS :, :128] = line
        out_ref[x, Z * ROWS :, 128:] = jnp.zeros((ROWS, width - 128), BF16)


def numbers_kernel(*refs):
    lines, out_ref = refs[:-1], refs[-1]
    total = jnp.zeros((ROWS, 128), F32)
    for x, ref in enumerate(lines):
        line = ref[:, :128].astype(F32)
        total = total + (pltpu.roll(line, LANES * C * x, 1) if x else line)
    out_ref[0, :, :128] = total.astype(BF16)
    out_ref[0, :, 128:] = jnp.zeros((ROWS, out_ref.shape[2] - 128), BF16)


def chosen(code, pieces):
    owned = pieces[0].shape[0]
    choice, local = code // owned, code % owned
    rows = jnp.zeros(pieces[0].shape[1:], BF16)
    for s, piece in enumerate(pieces):
        at = local if piece.shape[0] == owned else local % piece.shape[0]
        rows = jnp.where(choice == s, piece[at], rows)
    return rows


def code_of(ids_ref, x, z, core):
    return ids_ref[x, z, LANES * core + 3] * 32 + ids_ref[x, z, LANES * core + 4]


def pick_other_kernel(where_ref, ids_ref, f0, f1, f2a, f3, f2b, out_ref):
    core = 1 - where_ref[1]

    def step(z, carry):
        for x in range(X):
            code = code_of(ids_ref, x, z, core)
            out_ref[x * Z + z] = chosen(code, (f0, f1, f2a, f3, f2b))
        return carry

    lax.fori_loop(0, Z, step, 0, unroll=4)


def pick_own_kernel(where_ref, ids_ref, middle_ref, f0, f1, f2a, f3, f2b, out_ref):
    core = where_ref[1]
    middle_width = middle_ref.shape[2]

    def step(z, carry):
        for x in range(X):
            m = x * Z + z
            code = code_of(ids_ref, x, z, core)
            out_ref[m, :, :middle_width] = middle_ref[ids_ref[x, z, LANES * core]]
            out_ref[m, :, middle_width:] = chosen(code, (f0, f1, f2a, f3, f2b))
        return carry

    lax.fori_loop(0, Z, step, 0, unroll=4)


def merge_kernel(send_ref, extra_ref, out_ref):
    middle_width = send_ref.shape[2] - extra_ref.shape[2]
    out_ref[:, :, :middle_width] = send_ref[:, :, :middle_width]
    out_ref[:, :, middle_width:] = send_ref[:, :, middle_width:] + extra_ref[...]


def coarse_kernel(
    where_ref, ids_ref, x_ref, g_ref, ox_ref, og_ref, h0, h1, h2a, h2b, h3,
    s0, s1, s2a, s2b, s3, back_ref, other_back_ref, half_ref, own_term, other_term,
):
    y_index = where_ref[0]
    c_index, x_index, z_index = where_ref[1], where_ref[2], where_ref[3]
    own_id = ids_ref[x_index, z_index, LANES * c_index] // 16
    other_id = ids_ref[x_index, z_index, LANES * (1 - c_index)] // 16
    width = h0.shape[1] // 2

    def level(identity, inputs, upstream, term_ref, into_ref):
        choice = (y_index - identity + Y) % Y
        for s, ref in ((0, h0), (1, h1), (3, h3)):

            @pl.when(choice == s)
            def _(ref=ref):
                half_ref[...] = ref[...]

        @pl.when(choice == 2)
        def _():
            half_ref[: h2a.shape[0]] = h2a[...]
            half_ref[h2a.shape[0] :] = h2b[...]

        tokens, cotangent = inputs[...], upstream[...]
        before = dot(tokens, half_ref[:, :width], 1, 0)
        hidden_grad = dot(cotangent, half_ref[:, width:], 1, 0)
        hidden, before_grad = gelu_pair(before, hidden_grad)
        term_ref[:, :width] = dot(tokens, before_grad, 0, 0)
        term_ref[:, width:] = dot(cotangent, hidden, 0, 0)
        into_ref[...] = dot(before_grad, half_ref[:, :width], 1, 1).astype(into_ref.dtype)

    level(own_id, x_ref, g_ref, own_term, back_ref)
    level(other_id, ox_ref, og_ref, other_term, other_back_ref)
    middle_row = s2a.shape[0]
    everything = slice(0, s0.shape[0])
    lower, upper = slice(0, middle_row), slice(middle_row, s0.shape[0])
    for s, rows, ref in (
        (2, lower, s2a),
        (2, upper, s2b),
        (0, everything, s0),
        (1, everything, s1),
        (3, everything, s3),
    ):
        block = (y_index + s) % Y
        own, other = own_id == block, other_id == block

        @pl.when(jnp.logical_and(own, other))
        def _(ref=ref, rows=rows):
            ref[...] = (own_term[rows] + other_term[rows]).astype(BF16)

        @pl.when(jnp.logical_and(own, jnp.logical_not(other)))
        def _(ref=ref, rows=rows):
            ref[...] = own_term[rows].astype(BF16)

        @pl.when(jnp.logical_and(other, jnp.logical_not(own)))
        def _(ref=ref, rows=rows):
            ref[...] = other_term[rows].astype(BF16)

        @pl.when(jnp.logical_not(jnp.logical_or(own, other)))
        def _(ref=ref):
            ref[...] = jnp.zeros(ref.shape, BF16)


def coarse_relay_kernel(s1, s3, r1, r3, up_ref, down_ref):
    middle_row = r1.shape[0]
    up_ref[:middle_row] = (s1[:middle_row].astype(F32) + r1[...].astype(F32)).astype(BF16)
    up_ref[middle_row:] = s1[middle_row:]
    down_ref[:middle_row] = s3[:middle_row]
    down_ref[middle_row:] = (s3[middle_row:].astype(F32) + r3[...].astype(F32)).astype(BF16)


def coarse_sum_kernel(where_ref, s0, up_ref, down_ref, own_ref, *leaving):
    x_index = where_ref[2]
    rows = own_ref.shape[0]
    for s, ref in enumerate((own_ref,) + leaving):
        at = pl.ds(pl.multiple_of(((x_index + s) % X) * rows, rows), rows)
        total = s0[at].astype(F32) + up_ref[at].astype(F32) + down_ref[at].astype(F32)
        ref[...] = total.astype(ref.dtype)


def levels_kernel(x_ref, g_ref, w_ref, term_ref, back_ref):
    tokens, cotangent = x_ref[...], g_ref[...]
    middle = 256
    half = middle // 2
    before = dot(tokens, w_ref[:, :half], 1, 0)
    hidden_grad = dot(cotangent, w_ref[:, half:middle], 1, 0)
    hidden, before_grad = gelu_pair(before, hidden_grad)
    fine = w_ref[:, middle:]
    width = fine.shape[1]
    fine_before = dot(tokens, fine, 1, 0)
    fine_hidden_grad = pltpu.roll(dot(cotangent, fine, 1, 0), width // 2, 1)
    first = lax.broadcasted_iota(I32, fine_before.shape, 1) < width // 2
    fine_before = jnp.where(first, fine_before, 0.0)
    fine_hidden_grad = jnp.where(first, fine_hidden_grad, 0.0)
    fine_hidden, fine_before_grad = gelu_pair(fine_before, fine_hidden_grad)
    fine_hidden = pltpu.roll(fine_hidden.astype(F32), width // 2, 1).astype(BF16)
    term_ref[:, :half] = dot(tokens, before_grad, 0, 0).astype(BF16)
    term_ref[:, half:middle] = dot(cotangent, hidden, 0, 0).astype(BF16)
    term_ref[:, middle:] = (
        dot(tokens, fine_before_grad, 0, 0) + dot(cotangent, fine_hidden, 0, 0)
    ).astype(BF16)
    back_ref[...] = dot(before_grad, w_ref[:, :half], 1, 1) + dot(fine_before_grad, fine, 1, 1)


def collect_kernel(
    where_ref, ids_ref, numbers_ref, parts_ref, packet_ref, s0, s1, s3, sums_ref
):
    y_index, c_index = where_ref[0], where_ref[1]
    middle = parts_ref.shape[2] - 128
    slot = s0.shape[0]
    pairs = MEMBERS // 2
    sums_ref[...] = jnp.zeros(sums_ref.shape, F32)

    def step(zz, carry):
        for x in range(X):
            for h in range(2):
                z = 2 * zz + h
                block = ids_ref[x, z, LANES * c_index]
                place = ((block // slot - y_index + Y) % Y) * slot + block % slot
                m = x * Z + z
                sums_ref[place] = sums_ref[place] + parts_ref[m, :, :middle].astype(F32)
                pair = x * (Z // 2) + zz
                packet_ref[pair, :, h * 128 : h * 128 + 128] = parts_ref[m, :, middle:]
        return carry

    lax.fori_loop(0, Z // 2, step, 0)
    packet_ref[pairs] = numbers_ref[0]
    packet_ref[pairs + 1 :] = sums_ref[2 * slot : 3 * slot].astype(BF16)
    s0[...] = sums_ref[:slot]
    s1[...] = sums_ref[slot : 2 * slot]
    s3[...] = sums_ref[3 * slot :]


def relay_kernel(r1, r3, s1, s3, up_ref, down_ref):
    pairs = MEMBERS // 2
    lower = pairs // 2
    split = s1.shape[0] // 2
    middle = pairs + 1
    up_ref[:lower] = r1[:lower]
    up_ref[lower] = r1[pairs]
    up_ref[lower + 1 : lower + 1 + split] = (
        s1[:split] + r1[middle : middle + split].astype(F32)
    ).astype(BF16)
    up_ref[lower + 1 + split :] = s1[split:].astype(BF16)
    down_ref[:lower] = r3[lower:pairs]
    down_ref[lower : lower + split] = s3[:split].astype(BF16)
    down_ref[lower + split :] = (s3[split:] + r3[middle + split :].astype(F32)).astype(BF16)


def add_fine(where_ref, owned, ids_ref, p, piece, xs, sums_ref):
    y_index, c_index = where_ref[0], where_ref[1]

    def step(zz, carry):
        for x in xs:
            for h in range(2):
                place = LANES * (C * x + c_index)
                z = 2 * zz + h
                fine_id = ids_ref[p, z, place + 1] * 32 + ids_ref[p, z, place + 2]
                owner = fine_id // owned
                slot = ((owner + c_index) % C) * owned + fine_id % owned
                slot = jnp.where(owner // C == y_index, slot, C * owned)
                pair = (x - xs[0]) * (Z // 2) + zz
                part = piece[pair, :, h * 128 : h * 128 + 128]
                sums_ref[slot] = sums_ref[slot] + part.astype(F32)
        return carry

    lax.fori_loop(0, Z // 2, step, 0)


def first_fine_kernel(where_ref, ids_ref, p0, p1, p3, sums_ref):
    owned = (sums_ref.shape[0] - 8) // C
    sums_ref[...] = jnp.zeros(sums_ref.shape, F32)
    for p, piece in enumerate((p0, p1, p3)):
        add_fine(where_ref, owned, ids_ref, p, piece, range(X), sums_ref)


def middle_kernel(where_ref, s0, q1, q3, kept_ref, leave_ref):
    share = kept_ref.shape[0]
    lower = MEMBERS // 4

    def middle_of(side):
        low = side * share
        return (
            s0[pl.ds(low, share)]
            + q1[pl.ds(lower + 1 + low, share)].astype(F32)
            + q3[pl.ds(lower + low, share)].astype(F32)
        )

    kept_ref[...] = middle_of(where_ref[1])
    leave_ref[...] = middle_of(1 - where_ref[1]).astype(BF16)


def last_fine_kernel(
    where_ref, ids_ref, before_ref, q1, q3, leave_ref, fine_ref, sums_ref
):
    owned = fine_ref.shape[0]
    sums_ref[...] = before_ref[...]
    add_fine(where_ref, owned, ids_ref, 0, q1, range(X // 2), sums_ref)
    add_fine(where_ref, owned, ids_ref, 0, q3, range(X // 2, X), sums_ref)
    fine_ref[...] = sums_ref[:owned]
    half = owned // 2
    leave_ref[:, :, :128] = sums_ref[owned : owned + half].astype(BF16)
    leave_ref[:, :, 128:] = sums_ref[owned + half : 2 * owned].astype(BF16)


def coarse_done_kernel(coarse_ref, out_ref):
    coarse = coarse_ref[0].astype(F32)
    for z in range(1, Z):
        coarse = coarse + coarse_ref[z].astype(F32)
    out_ref[...] = coarse.astype(BF16)


def done_kernel(kept_ref, arrived_ref, coarse_ref, out_ref):
    share = kept_ref.shape[0]
    middle = (kept_ref[...] + arrived_ref[...].astype(F32)).astype(BF16)
    coarse = coarse_ref[...]
    for g in range(out_ref.shape[0]):
        out_ref[g, :share] = middle
        out_ref[g, share] = coarse


def finish_kernel(fine_ref, arrived_ref, out_ref):
    half = fine_ref.shape[0] // 2
    for h in range(2):
        low = h * half
        out_ref[low : low + half] = (
            fine_ref[low : low + half]
            + arrived_ref[:, :, h * 128 : h * 128 + 128].astype(F32)
        ).astype(BF16)


def spread_kernel(total_ref, coarse_ref, middle_ref):
    share = total_ref.shape[1] - 1
    width = total_ref.shape[3] // 2
    for y in range(Y):
        for core in range(C):
            g = y * C + core
            middle_ref[g * share : (g + 1) * share] = total_ref[g, :share]
            low = core * width
            coarse_ref[y, :, low : low + width] = total_ref[g, share, :, :width]
            low = (C + core) * width
            coarse_ref[y, :, low : low + width] = total_ref[g, share, :, width:]


def on_device(tokens, cotangent, path, coarse_weights, middle_weights, fine_weights):
    y_index, c_index = lax.axis_index("y"), lax.axis_index("c")
    x_index = lax.axis_index("x")
    where = jnp.stack([y_index, c_index, x_index, lax.axis_index("z")]).astype(I32)
    fine_owned, _, fine_width = fine_weights.shape
    coarse_width = coarse_weights.shape[2]
    middle_width = middle_weights.shape[2]
    half = coarse_width // 2
    depth = MEMBERS * ROWS

    other_path = shift(path, "c", 1)
    packet = kernel_call(
        partial(packet_kernel, fine_owned),
        [SMEM, SMEM, SMEM, VMEM],
        bf16(Z, ROWS, half + 128),
    )(where, path, other_path, coarse_weights)
    packets = exchange(packet, "z")

    fine_one = shift(fine_weights, "y", 1)
    fine_three = shift(after(fine_weights, packet), "y", 3)
    split = fine_owned // 2
    fine_two = shift(fine_one[:split], "y", 1)
    packets, fine_one, fine_two, fine_three = lax.optimization_barrier((packets, fine_one, fine_two, fine_three))
    packets = kernel_call(repack_kernel, [VMEM], bf16(X, Z * ROWS + ROWS, half))(packets)
    packets = exchange(packets, "x")
    fine_rows = [
        fine_weights,
        fine_one,
        fine_two,
        fine_three,
        shift(fine_three[split:], "y", 3),
    ]
    ids = packets[:, Z * ROWS : Z * ROWS + Z, : LANES * C].astype(I32)
    extra = kernel_call(
        pick_other_kernel, [SMEM] * 2 + [VMEM] * 5, bf16(MEMBERS, ROWS, fine_width)
    )(where, ids, *fine_rows)
    arrived = shift(extra, "c", 1)
    send = kernel_call(
        pick_own_kernel,
        [SMEM] * 2 + [VMEM] * 6,
        bf16(MEMBERS, ROWS, middle_width + fine_width),
    )(where, ids, middle_weights, *fine_rows)
    send = kernel_call(merge_kernel, [VMEM] * 2, bf16(*send.shape))(send, arrived)
    mine = exchange(send, ("x", "z")).reshape(depth, -1)

    both = jnp.concatenate([after(tokens, send), cotangent], axis=0)
    other_both = shift(both, "c", 1)

    lines = after(packets, send)[:, Z * ROWS :]
    numbers = kernel_call(numbers_kernel, [VMEM] * X, bf16(1, ROWS, 2 * fine_width))(
        *[lines[x] for x in range(X)]
    )
    block = after(packets, send)[:, : Z * ROWS].reshape(depth, half)
    one, three = shift(block, "y", 1), shift(block, "y", 3)
    middle_row = depth // 2
    halves = [
        block,
        one,
        shift(one[:middle_row], "y", 1),
        shift(three[middle_row:], "y", 3),
        three,
    ]
    length = tokens.shape[0]
    slots = kernel_call(
        coarse_kernel,
        [SMEM, SMEM] + [VMEM] * 9,
        tuple(
            [bf16(depth, half)] * 2
            + [bf16(middle_row, half)] * 2
            + [bf16(depth, half)]
            + [bf16(length, depth)] * 2
        ),
        [
            pltpu.VMEM((depth, half), BF16),
            pltpu.VMEM((depth, half), F32),
            pltpu.VMEM((depth, half), F32),
        ],
        cost=10_000_000,
    )(
        where, ids, tokens, cotangent, other_both[:length], other_both[length:], *halves
    )
    near, ahead, far_low, far_high, behind, coarse_back, other_back = slots
    up, down = shift(far_low, "y", 1), shift(far_high, "y", 3)
    mine, numbers, up = lax.optimization_barrier((mine, numbers, up))

    terms, back = kernel_call(
        levels_kernel,
        [VMEM] * 3,
        (bf16(depth, middle_width + fine_width), f32(length, depth)),
        cost=10_000_000,
    )(tokens, cotangent, mine)
    parts = exchange(terms.reshape(MEMBERS, ROWS, -1), ("x", "z"))

    up, down = kernel_call(coarse_relay_kernel, [VMEM] * 4, (bf16(depth, half),) * 2)(
        ahead, behind, up, down
    )
    up, down = shift(after(up, terms), "y", 1), shift(after(down, terms), "y", 3)
    column_sum, *leaving = kernel_call(
        coarse_sum_kernel,
        [SMEM] + [VMEM] * 3,
        tuple([f32(Z * ROWS, half)] + [bf16(Z * ROWS, half)] * (X - 1)),
    )(where, near, up, down)
    for s in range(1, X):
        column_sum = column_sum + shift(leaving[s - 1], "x", s).astype(F32)
    column_sum = column_sum.astype(BF16).reshape(Z, ROWS, half)
    other_back = shift(after(other_back, terms), "c", 1)
    parts, column_sum, other_back = lax.optimization_barrier((parts, column_sum, other_back))

    middle_count = middle_weights.shape[0]
    pairs = MEMBERS // 2
    lower = pairs // 2
    quarter_count = middle_count // Y
    share = quarter_count // C
    first, s0, s1, s3 = kernel_call(
        collect_kernel,
        [SMEM, SMEM, VMEM, VMEM],
        tuple(
            [bf16(pairs + 1 + quarter_count, ROWS, middle_width)]
            + [f32(quarter_count, ROWS, middle_width)] * 3
        ),
        [pltpu.VMEM((middle_count, ROWS, middle_width), F32)],
    )(where, ids, numbers, parts)
    r1, r3 = shift(first, "y", 1), shift(first, "y", 3)
    coarse_four = exchange(after(column_sum, first), "z")
    second = kernel_call(
        relay_kernel,
        [VMEM] * 4,
        (
            bf16(lower + 1 + quarter_count, ROWS, middle_width),
            bf16(lower + quarter_count, ROWS, middle_width),
        ),
    )(r1, r3, s1, s3)
    q1, q3 = shift(second[0], "y", 1), shift(second[1], "y", 3)
    fine_ids = [f[pairs, :Z, : LANES * C * X].astype(I32) for f in (first, r1, r3)]
    fine_sums = kernel_call(
        first_fine_kernel,
        [SMEM, SMEM] + [VMEM] * 3,
        f32(C * fine_owned + 8, ROWS, fine_width),
    )(where, jnp.stack(fine_ids), first, r1, r3)
    fine_sums, q1, q3, coarse_four = lax.optimization_barrier(
        (fine_sums, q1, q3, coarse_four)
    )
    middle_kept, middle_leave = kernel_call(
        middle_kernel,
        [SMEM] + [VMEM] * 3,
        (f32(share, ROWS, middle_width), bf16(share, ROWS, middle_width)),
    )(where, s0, q1, q3)
    middle_arrived = shift(middle_leave, "c", 1)
    fine_leave, fine_kept = kernel_call(
        last_fine_kernel,
        [SMEM, SMEM] + [VMEM] * 3,
        (bf16(fine_owned // 2, ROWS, 2 * fine_width), f32(fine_owned, ROWS, fine_width)),
        [pltpu.VMEM((C * fine_owned + 8, ROWS, fine_width), F32)],
    )(where, q1[lower, :Z, : LANES * C * X].astype(I32)[None], fine_sums, q1, q3)
    coarse_done = kernel_call(coarse_done_kernel, [VMEM], bf16(ROWS, half))(coarse_four)
    done = kernel_call(
        done_kernel, [VMEM] * 3, bf16(Y * C, share + 1, ROWS, middle_width)
    )(middle_kept, middle_arrived, coarse_done)
    total = exchange(done, ("y", "c"))
    fine_arrived = shift(after(fine_leave, done), "c", 1)
    coarse_total, middle_total = kernel_call(
        spread_kernel, [VMEM], (bf16(*coarse_weights.shape), bf16(*middle_weights.shape))
    )(total)
    fine_total = kernel_call(
        finish_kernel, [VMEM] * 2, bf16(fine_owned, ROWS, fine_width)
    )(fine_kept, fine_arrived)
    tokens_grad = (coarse_back.astype(F32) + other_back.astype(F32) + back).astype(BF16)
    return (tokens_grad, coarse_total, middle_total, fine_total)


def solution(mesh):
    fine_mesh = Mesh(mesh.devices.reshape(Y, C, X, Z), EVERYONE)
    members = ("x", "z")
    return jax.shard_map(
        on_device,
        mesh=fine_mesh,
        in_specs=(
            P(EVERYONE, None),
            P(EVERYONE, None),
            P(EVERYONE, None),
            P(None, members, None),
            P(None, members, None),
            P(("y", "c"), members, None),
        ),
        out_specs=(
            P(EVERYONE, None),
            P(None, members, None),
            P(None, members, None),
            P(("y", "c"), members, None),
        ),
        check_vma=False,
    )
```

```python
from functools import partial

import jax
import jax.numpy as jnp
from jax import lax
from jax.experimental import pallas as pl
from jax.experimental.pallas import tpu as pltpu
from jax.sharding import Mesh, PartitionSpec as P

F32 = jnp.float32
BF16 = jnp.bfloat16
I32 = jnp.int32
Y, C, X, Z = 4, 2, 4, 16
MEMBERS = X * Z
ROWS = 16
LANES = 8
EVERYONE = ("y", "c", "x", "z")
VMEM = pl.BlockSpec(memory_space=pltpu.VMEM)
SMEM = pl.BlockSpec(memory_space=pltpu.SMEM)


def exchange(array, axes):
    return lax.all_to_all(array, axes, split_axis=0, concat_axis=0, tiled=True)


def gather(array, axes):
    count = lax.axis_size(axes)
    return exchange(jnp.broadcast_to(array[None], (count,) + array.shape), axes)


def shift(array, axis, step):
    count = lax.axis_size(axis)
    return lax.ppermute(array, axis, [(i, (i + step) % count) for i in range(count)])


def after(array, *others):
    return lax.optimization_barrier((array,) + others)[0]


def kernel_call(body, in_specs, out_shape, scratch=(), cost=1_000_000, limit=16):
    return pl.pallas_call(
        body,
        out_shape=out_shape,
        in_specs=in_specs,
        out_specs=jax.tree.map(lambda _: VMEM, out_shape),
        scratch_shapes=list(scratch),
        compiler_params=pltpu.CompilerParams(vmem_limit_bytes=limit * 1024 * 1024),
        cost_estimate=pl.CostEstimate(flops=cost, bytes_accessed=cost, transcendentals=0),
    )


def bf16(*shape):
    return jax.ShapeDtypeStruct(shape, BF16)


def f32(*shape):
    return jax.ShapeDtypeStruct(shape, F32)


def dot(left, right, left_dim, right_dim):
    return lax.dot_general(
        left, right, (((left_dim,), (right_dim,)), ((), ())), preferred_element_type=F32
    )


def gelu_pair(v, upstream):
    scale = 0.7978845608028654
    square = v * v
    t = jnp.tanh(scale * (v + 0.044715 * (square * v)))
    half = 0.5 * (1.0 + t)
    slope = half + 0.5 * v * (1.0 - t * t) * (scale * (1.0 + 0.134145 * square))
    return (v * half).astype(BF16), (upstream * slope).astype(BF16)


def packet_kernel(owned, where_ref, own_ref, other_ref, coarse_ref, out_ref):
    y_index, c_index = where_ref[0], where_ref[1]
    width = coarse_ref.shape[2] // 4
    up = coarse_ref[y_index, :, pl.ds(pl.multiple_of(c_index * width, width), width)]
    down = coarse_ref[
        y_index, :, pl.ds(pl.multiple_of((c_index + 2) * width, width), width)
    ]
    lanes = lax.broadcasted_iota(I32, (ROWS, 128), 1)
    numbers = jnp.zeros((ROWS, 128), F32)
    for core, ref in ((c_index, own_ref), (1 - c_index, other_ref)):
        fine_id = ref[0, 2]
        owner, slot = fine_id // owned, fine_id % owned
        choice = (y_index - owner // C + Y) % Y
        choice = jnp.where(jnp.logical_and(choice == 2, slot >= owned // 2), Y, choice)
        choice = jnp.where(owner % C == c_index, choice, Y + 1)
        code = choice * owned + slot
        values = (ref[0, 1], fine_id // 32, fine_id % 32, code // 32, code % 32)
        for i, value in enumerate(values):
            numbers = jnp.where(lanes == LANES * core + i, value.astype(F32), numbers)
    numbers = numbers.astype(BF16)
    for z in range(Z):
        out_ref[z, :, :width] = up
        out_ref[z, :, width : 2 * width] = down
        out_ref[z, :, 2 * width :] = numbers


def repack_kernel(packets_ref, out_ref):
    width = out_ref.shape[2]
    rows = lax.broadcasted_iota(I32, (ROWS, 128), 0)
    line = jnp.zeros((ROWS, 128), F32)
    for z in range(Z):
        line = jnp.where(rows == z, packets_ref[z, :, width:].astype(F32), line)
    line = line.astype(BF16)
    for x in range(X):
        for z in range(Z):
            out_ref[x, z * ROWS : (z + 1) * ROWS] = packets_ref[z, :, :width]
        out_ref[x, Z * ROWS :, :128] = line
        out_ref[x, Z * ROWS :, 128:] = jnp.zeros((ROWS, width - 128), BF16)


def numbers_kernel(*refs):
    lines, out_ref = refs[:-1], refs[-1]
    total = jnp.zeros((ROWS, 128), F32)
    for x, ref in enumerate(lines):
        line = ref[:, :128].astype(F32)
        total = total + (pltpu.roll(line, LANES * C * x, 1) if x else line)
    out_ref[0, :, :128] = total.astype(BF16)
    out_ref[0, :, 128:] = jnp.zeros((ROWS, out_ref.shape[2] - 128), BF16)


def chosen(code, pieces):
    owned = pieces[0].shape[0]
    choice, local = code // owned, code % owned
    rows = jnp.zeros(pieces[0].shape[1:], BF16)
    for s, piece in enumerate(pieces):
        at = local if piece.shape[0] == owned else local % piece.shape[0]
        rows = jnp.where(choice == s, piece[at], rows)
    return rows


def code_of(ids_ref, x, z, core):
    return ids_ref[x, z, LANES * core + 3] * 32 + ids_ref[x, z, LANES * core + 4]


def pick_other_kernel(where_ref, ids_ref, f0, f1, f2a, f3, f2b, out_ref):
    core = 1 - where_ref[1]

    def step(z, carry):
        for x in range(X):
            code = code_of(ids_ref, x, z, core)
            out_ref[x * Z + z] = chosen(code, (f0, f1, f2a, f3, f2b))
        return carry

    lax.fori_loop(0, Z, step, 0, unroll=4)


def pick_own_kernel(where_ref, ids_ref, middle_ref, f0, f1, f2a, f3, f2b, out_ref):
    core = where_ref[1]
    middle_width = middle_ref.shape[2]

    def step(z, carry):
        for x in range(X):
            m = x * Z + z
            code = code_of(ids_ref, x, z, core)
            out_ref[m, :, :middle_width] = middle_ref[ids_ref[x, z, LANES * core]]
            out_ref[m, :, middle_width:] = chosen(code, (f0, f1, f2a, f3, f2b))
        return carry

    lax.fori_loop(0, Z, step, 0, unroll=4)


def merge_kernel(send_ref, extra_ref, out_ref):
    middle_width = send_ref.shape[2] - extra_ref.shape[2]
    out_ref[:, :, :middle_width] = send_ref[:, :, :middle_width]
    out_ref[:, :, middle_width:] = send_ref[:, :, middle_width:] + extra_ref[...]


def coarse_kernel(
    where_ref, ids_ref, x_ref, g_ref, ox_ref, og_ref, h0, h1, h2a, h2b, h3,
    s0, s1, s2a, s2b, s3, back_ref, other_back_ref, half_ref, own_term, other_term,
):
    y_index = where_ref[0]
    c_index, x_index, z_index = where_ref[1], where_ref[2], where_ref[3]
    own_id = ids_ref[x_index, z_index, LANES * c_index] // 16
    other_id = ids_ref[x_index, z_index, LANES * (1 - c_index)] // 16
    width = h0.shape[1] // 2

    def level(identity, inputs, upstream, term_ref, into_ref):
        choice = (y_index - identity + Y) % Y
        for s, ref in ((0, h0), (1, h1), (3, h3)):

            @pl.when(choice == s)
            def _(ref=ref):
                half_ref[...] = ref[...]

        @pl.when(choice == 2)
        def _():
            half_ref[: h2a.shape[0]] = h2a[...]
            half_ref[h2a.shape[0] :] = h2b[...]

        tokens, cotangent = inputs[...], upstream[...]
        before = dot(tokens, half_ref[:, :width], 1, 0)
        hidden_grad = dot(cotangent, half_ref[:, width:], 1, 0)
        hidden, before_grad = gelu_pair(before, hidden_grad)
        term_ref[:, :width] = dot(tokens, before_grad, 0, 0)
        term_ref[:, width:] = dot(cotangent, hidden, 0, 0)
        into_ref[...] = dot(before_grad, half_ref[:, :width], 1, 1).astype(into_ref.dtype)

    level(own_id, x_ref, g_ref, own_term, back_ref)
    level(other_id, ox_ref, og_ref, other_term, other_back_ref)
    middle_row = s2a.shape[0]
    everything = slice(0, s0.shape[0])
    lower, upper = slice(0, middle_row), slice(middle_row, s0.shape[0])
    for s, rows, ref in (
        (2, lower, s2a),
        (2, upper, s2b),
        (0, everything, s0),
        (1, everything, s1),
        (3, everything, s3),
    ):
        block = (y_index + s) % Y
        own, other = own_id == block, other_id == block

        @pl.when(jnp.logical_and(own, other))
        def _(ref=ref, rows=rows):
            ref[...] = (own_term[rows] + other_term[rows]).astype(BF16)

        @pl.when(jnp.logical_and(own, jnp.logical_not(other)))
        def _(ref=ref, rows=rows):
            ref[...] = own_term[rows].astype(BF16)

        @pl.when(jnp.logical_and(other, jnp.logical_not(own)))
        def _(ref=ref, rows=rows):
            ref[...] = other_term[rows].astype(BF16)

        @pl.when(jnp.logical_not(jnp.logical_or(own, other)))
        def _(ref=ref):
            ref[...] = jnp.zeros(ref.shape, BF16)


def coarse_relay_kernel(s1, s3, r1, r3, up_ref, down_ref):
    middle_row = r1.shape[0]
    up_ref[:middle_row] = (s1[:middle_row].astype(F32) + r1[...].astype(F32)).astype(BF16)
    up_ref[middle_row:] = s1[middle_row:]
    down_ref[:middle_row] = s3[:middle_row]
    down_ref[middle_row:] = (s3[middle_row:].astype(F32) + r3[...].astype(F32)).astype(BF16)


def coarse_sum_kernel(where_ref, s0, up_ref, down_ref, own_ref, *leaving):
    x_index = where_ref[2]
    rows = own_ref.shape[0]
    for s, ref in enumerate((own_ref,) + leaving):
        at = pl.ds(pl.multiple_of(((x_index + s) % X) * rows, rows), rows)
        total = s0[at].astype(F32) + up_ref[at].astype(F32) + down_ref[at].astype(F32)
        ref[...] = total.astype(ref.dtype)


def levels_kernel(x_ref, g_ref, w_ref, term_ref, back_ref):
    tokens, cotangent = x_ref[...], g_ref[...]
    middle = 256
    half = middle // 2
    before = dot(tokens, w_ref[:, :half], 1, 0)
    hidden_grad = dot(cotangent, w_ref[:, half:middle], 1, 0)
    hidden, before_grad = gelu_pair(before, hidden_grad)
    fine = w_ref[:, middle:]
    width = fine.shape[1]
    fine_before = dot(tokens, fine, 1, 0)
    fine_hidden_grad = pltpu.roll(dot(cotangent, fine, 1, 0), width // 2, 1)
    first = lax.broadcasted_iota(I32, fine_before.shape, 1) < width // 2
    fine_before = jnp.where(first, fine_before, 0.0)
    fine_hidden_grad = jnp.where(first, fine_hidden_grad, 0.0)
    fine_hidden, fine_before_grad = gelu_pair(fine_before, fine_hidden_grad)
    fine_hidden = pltpu.roll(fine_hidden.astype(F32), width // 2, 1).astype(BF16)
    term_ref[:, :half] = dot(tokens, before_grad, 0, 0).astype(BF16)
    term_ref[:, half:middle] = dot(cotangent, hidden, 0, 0).astype(BF16)
    term_ref[:, middle:] = (
        dot(tokens, fine_before_grad, 0, 0) + dot(cotangent, fine_hidden, 0, 0)
    ).astype(BF16)
    back_ref[...] = dot(before_grad, w_ref[:, :half], 1, 1) + dot(fine_before_grad, fine, 1, 1)


def collect_kernel(
    where_ref, ids_ref, numbers_ref, parts_ref, packet_ref, s0, s1, s3, sums_ref
):
    y_index, c_index = where_ref[0], where_ref[1]
    middle = parts_ref.shape[2] - 128
    slot = s0.shape[0]
    pairs = MEMBERS // 2
    sums_ref[...] = jnp.zeros(sums_ref.shape, F32)

    def step(zz, carry):
        for x in range(X):
            for h in range(2):
                z = 2 * zz + h
                block = ids_ref[x, z, LANES * c_index]
                place = ((block // slot - y_index + Y) % Y) * slot + block % slot
                m = x * Z + z
                sums_ref[place] = sums_ref[place] + parts_ref[m, :, :middle].astype(F32)
                pair = x * (Z // 2) + zz
                packet_ref[pair, :, h * 128 : h * 128 + 128] = parts_ref[m, :, middle:]
        return carry

    lax.fori_loop(0, Z // 2, step, 0)
    packet_ref[pairs] = numbers_ref[0]
    packet_ref[pairs + 1 :] = sums_ref[2 * slot : 3 * slot].astype(BF16)
    s0[...] = sums_ref[:slot]
    s1[...] = sums_ref[slot : 2 * slot]
    s3[...] = sums_ref[3 * slot :]


def relay_kernel(r1, r3, s1, s3, up_ref, down_ref):
    pairs = MEMBERS // 2
    lower = pairs // 2
    split = s1.shape[0] // 2
    middle = pairs + 1
    up_ref[:lower] = r1[:lower]
    up_ref[lower] = r1[pairs]
    up_ref[lower + 1 : lower + 1 + split] = (
        s1[:split] + r1[middle : middle + split].astype(F32)
    ).astype(BF16)
    up_ref[lower + 1 + split :] = s1[split:].astype(BF16)
    down_ref[:lower] = r3[lower:pairs]
    down_ref[lower : lower + split] = s3[:split].astype(BF16)
    down_ref[lower + split :] = (s3[split:] + r3[middle + split :].astype(F32)).astype(BF16)


def add_fine(where_ref, owned, ids_ref, p, piece, xs, sums_ref):
    y_index, c_index = where_ref[0], where_ref[1]

    def step(zz, carry):
        for x in xs:
            for h in range(2):
                place = LANES * (C * x + c_index)
                z = 2 * zz + h
                fine_id = ids_ref[p, z, place + 1] * 32 + ids_ref[p, z, place + 2]
                owner = fine_id // owned
                slot = ((owner + c_index) % C) * owned + fine_id % owned
                slot = jnp.where(owner // C == y_index, slot, C * owned)
                pair = (x - xs[0]) * (Z // 2) + zz
                part = piece[pair, :, h * 128 : h * 128 + 128]
                sums_ref[slot] = sums_ref[slot] + part.astype(F32)
        return carry

    lax.fori_loop(0, Z // 2, step, 0)


def first_fine_kernel(where_ref, ids_ref, p0, p1, p3, sums_ref):
    owned = (sums_ref.shape[0] - 8) // C
    sums_ref[...] = jnp.zeros(sums_ref.shape, F32)
    for p, piece in enumerate((p0, p1, p3)):
        add_fine(where_ref, owned, ids_ref, p, piece, range(X), sums_ref)


def middle_kernel(where_ref, s0, q1, q3, kept_ref, leave_ref):
    share = kept_ref.shape[0]
    lower = MEMBERS // 4

    def middle_of(side):
        low = side * share
        return (
            s0[pl.ds(low, share)]
            + q1[pl.ds(lower + 1 + low, share)].astype(F32)
            + q3[pl.ds(lower + low, share)].astype(F32)
        )

    kept_ref[...] = middle_of(where_ref[1])
    leave_ref[...] = middle_of(1 - where_ref[1]).astype(BF16)


def last_fine_kernel(
    where_ref, ids_ref, before_ref, q1, q3, leave_ref, fine_ref, sums_ref
):
    owned = fine_ref.shape[0]
    sums_ref[...] = before_ref[...]
    add_fine(where_ref, owned, ids_ref, 0, q1, range(X // 2), sums_ref)
    add_fine(where_ref, owned, ids_ref, 0, q3, range(X // 2, X), sums_ref)
    fine_ref[...] = sums_ref[:owned]
    half = owned // 2
    leave_ref[:, :, :128] = sums_ref[owned : owned + half].astype(BF16)
    leave_ref[:, :, 128:] = sums_ref[owned + half : 2 * owned].astype(BF16)


def coarse_done_kernel(coarse_ref, out_ref):
    coarse = coarse_ref[0].astype(F32)
    for z in range(1, Z):
        coarse = coarse + coarse_ref[z].astype(F32)
    out_ref[...] = coarse.astype(BF16)


def done_kernel(kept_ref, arrived_ref, coarse_ref, out_ref):
    share = kept_ref.shape[0]
    middle = (kept_ref[...] + arrived_ref[...].astype(F32)).astype(BF16)
    coarse = coarse_ref[...]
    for g in range(out_ref.shape[0]):
        out_ref[g, :share] = middle
        out_ref[g, share] = coarse


def finish_kernel(fine_ref, arrived_ref, out_ref):
    half = fine_ref.shape[0] // 2
    for h in range(2):
        low = h * half
        out_ref[low : low + half] = (
            fine_ref[low : low + half]
            + arrived_ref[:, :, h * 128 : h * 128 + 128].astype(F32)
        ).astype(BF16)


def spread_kernel(total_ref, coarse_ref, middle_ref):
    share = total_ref.shape[1] - 1
    width = total_ref.shape[3] // 2
    for y in range(Y):
        for core in range(C):
            g = y * C + core
            middle_ref[g * share : (g + 1) * share] = total_ref[g, :share]
            low = core * width
            coarse_ref[y, :, low : low + width] = total_ref[g, share, :, :width]
            low = (C + core) * width
            coarse_ref[y, :, low : low + width] = total_ref[g, share, :, width:]


def on_device(tokens, cotangent, path, coarse_weights, middle_weights, fine_weights):
    y_index, c_index = lax.axis_index("y"), lax.axis_index("c")
    x_index = lax.axis_index("x")
    where = jnp.stack([y_index, c_index, x_index, lax.axis_index("z")]).astype(I32)
    fine_owned, _, fine_width = fine_weights.shape
    coarse_width = coarse_weights.shape[2]
    middle_width = middle_weights.shape[2]
    half = coarse_width // 2
    depth = MEMBERS * ROWS

    other_path = shift(path, "c", 1)
    packet = kernel_call(
        partial(packet_kernel, fine_owned),
        [SMEM, SMEM, SMEM, VMEM],
        bf16(Z, ROWS, half + 128),
    )(where, path, other_path, coarse_weights)
    packets = exchange(packet, "z")

    fine_one = shift(fine_weights, "y", 1)
    fine_three = shift(after(fine_weights, packet), "y", 3)
    split = fine_owned // 2
    fine_two = shift(fine_one[:split], "y", 1)
    packets, fine_one, fine_two, fine_three = lax.optimization_barrier((packets, fine_one, fine_two, fine_three))
    packets = kernel_call(repack_kernel, [VMEM], bf16(X, Z * ROWS + ROWS, half))(packets)
    packets = exchange(packets, "x")
    fine_rows = [
        fine_weights,
        fine_one,
        fine_two,
        fine_three,
        shift(fine_three[split:], "y", 3),
    ]
    ids = packets[:, Z * ROWS : Z * ROWS + Z, : LANES * C].astype(I32)
    extra = kernel_call(
        pick_other_kernel, [SMEM] * 2 + [VMEM] * 5, bf16(MEMBERS, ROWS, fine_width)
    )(where, ids, *fine_rows)
    arrived = shift(extra, "c", 1)
    send = kernel_call(
        pick_own_kernel,
        [SMEM] * 2 + [VMEM] * 6,
        bf16(MEMBERS, ROWS, middle_width + fine_width),
    )(where, ids, middle_weights, *fine_rows)
    send = kernel_call(merge_kernel, [VMEM] * 2, bf16(*send.shape))(send, arrived)
    mine = exchange(send, ("x", "z")).reshape(depth, -1)

    both = jnp.concatenate([after(tokens, send), cotangent], axis=0)
    other_both = shift(both, "c", 1)

    lines = after(packets, send)[:, Z * ROWS :]
    numbers = kernel_call(numbers_kernel, [VMEM] * X, bf16(1, ROWS, 2 * fine_width))(
        *[lines[x] for x in range(X)]
    )
    block = after(packets, send)[:, : Z * ROWS].reshape(depth, half)
    one, three = shift(block, "y", 1), shift(block, "y", 3)
    middle_row = depth // 2
    halves = [
        block,
        one,
        shift(one[:middle_row], "y", 1),
        shift(three[middle_row:], "y", 3),
        three,
    ]
    length = tokens.shape[0]
    slots = kernel_call(
        coarse_kernel,
        [SMEM, SMEM] + [VMEM] * 9,
        tuple(
            [bf16(depth, half)] * 2
            + [bf16(middle_row, half)] * 2
            + [bf16(depth, half)]
            + [bf16(length, depth)] * 2
        ),
        [
            pltpu.VMEM((depth, half), BF16),
            pltpu.VMEM((depth, half), F32),
            pltpu.VMEM((depth, half), F32),
        ],
        cost=10_000_000,
    )(
        where, ids, tokens, cotangent, other_both[:length], other_both[length:], *halves
    )
    near, ahead, far_low, far_high, behind, coarse_back, other_back = slots
    up, down = shift(far_low, "y", 1), shift(far_high, "y", 3)
    mine, numbers, up, down = lax.optimization_barrier((mine, numbers, up, down))

    terms, back = kernel_call(
        levels_kernel,
        [VMEM] * 3,
        (bf16(depth, middle_width + fine_width), f32(length, depth)),
        cost=10_000_000,
    )(tokens, cotangent, mine)
    parts = exchange(terms.reshape(MEMBERS, ROWS, -1), ("x", "z"))

    up, down = kernel_call(coarse_relay_kernel, [VMEM] * 4, (bf16(depth, half),) * 2)(
        ahead, behind, up, down
    )
    up, down = shift(after(up, terms), "y", 1), shift(after(down, terms), "y", 3)
    column_sum, *leaving = kernel_call(
        coarse_sum_kernel,
        [SMEM] + [VMEM] * 3,
        tuple([f32(Z * ROWS, half)] + [bf16(Z * ROWS, half)] * (X - 1)),
    )(where, near, up, down)
    for s in range(1, X):
        column_sum = column_sum + shift(leaving[s - 1], "x", s).astype(F32)
    column_sum = column_sum.astype(BF16).reshape(Z, ROWS, half)
    other_back = shift(after(other_back, terms), "c", 1)
    parts, column_sum, other_back = lax.optimization_barrier((parts, column_sum, other_back))

    middle_count = middle_weights.shape[0]
    pairs = MEMBERS // 2
    lower = pairs // 2
    quarter_count = middle_count // Y
    share = quarter_count // C
    first, s0, s1, s3 = kernel_call(
        collect_kernel,
        [SMEM, SMEM, VMEM, VMEM],
        tuple(
            [bf16(pairs + 1 + quarter_count, ROWS, middle_width)]
            + [f32(quarter_count, ROWS, middle_width)] * 3
        ),
        [pltpu.VMEM((middle_count, ROWS, middle_width), F32)],
    )(where, ids, numbers, parts)
    r1, r3 = shift(first, "y", 1), shift(first, "y", 3)
    coarse_four = exchange(after(column_sum, first), "z")
    second = kernel_call(
        relay_kernel,
        [VMEM] * 4,
        (
            bf16(lower + 1 + quarter_count, ROWS, middle_width),
            bf16(lower + quarter_count, ROWS, middle_width),
        ),
    )(r1, r3, s1, s3)
    q1, q3 = shift(second[0], "y", 1), shift(second[1], "y", 3)
    fine_ids = [f[pairs, :Z, : LANES * C * X].astype(I32) for f in (first, r1, r3)]
    fine_sums = kernel_call(
        first_fine_kernel,
        [SMEM, SMEM] + [VMEM] * 3,
        f32(C * fine_owned + 8, ROWS, fine_width),
    )(where, jnp.stack(fine_ids), first, r1, r3)
    fine_sums, q1, q3, coarse_four = lax.optimization_barrier(
        (fine_sums, q1, q3, coarse_four)
    )
    middle_kept, middle_leave = kernel_call(
        middle_kernel,
        [SMEM] + [VMEM] * 3,
        (f32(share, ROWS, middle_width), bf16(share, ROWS, middle_width)),
    )(where, s0, q1, q3)
    middle_arrived = shift(middle_leave, "c", 1)
    fine_leave, fine_kept = kernel_call(
        last_fine_kernel,
        [SMEM, SMEM] + [VMEM] * 3,
        (bf16(fine_owned // 2, ROWS, 2 * fine_width), f32(fine_owned, ROWS, fine_width)),
        [pltpu.VMEM((C * fine_owned + 8, ROWS, fine_width), F32)],
    )(where, q1[lower, :Z, : LANES * C * X].astype(I32)[None], fine_sums, q1, q3)
    coarse_done = kernel_call(coarse_done_kernel, [VMEM], bf16(ROWS, half))(coarse_four)
    done = kernel_call(
        done_kernel, [VMEM] * 3, bf16(Y * C, share + 1, ROWS, middle_width)
    )(middle_kept, middle_arrived, coarse_done)
    total = exchange(done, ("y", "c"))
    fine_arrived = shift(after(fine_leave, done), "c", 1)
    coarse_total, middle_total = kernel_call(
        spread_kernel, [VMEM], (bf16(*coarse_weights.shape), bf16(*middle_weights.shape))
    )(total)
    fine_total = kernel_call(
        finish_kernel, [VMEM] * 2, bf16(fine_owned, ROWS, fine_width)
    )(fine_kept, fine_arrived)
    tokens_grad = (coarse_back.astype(F32) + other_back.astype(F32) + back).astype(BF16)
    return (tokens_grad, coarse_total, middle_total, fine_total)


def solution(mesh):
    fine_mesh = Mesh(mesh.devices.reshape(Y, C, X, Z), EVERYONE)
    members = ("x", "z")
    return jax.shard_map(
        on_device,
        mesh=fine_mesh,
        in_specs=(
            P(EVERYONE, None),
            P(EVERYONE, None),
            P(EVERYONE, None),
            P(None, members, None),
            P(None, members, None),
            P(("y", "c"), members, None),
        ),
        out_specs=(
            P(EVERYONE, None),
            P(None, members, None),
            P(None, members, None),
            P(("y", "c"), members, None),
        ),
        check_vma=False,
    )
```
